256 devices in a mesh: seq: 32 (over y, z), chan: 8 (over x, core).
Axes of the slice: x: 4, y: 4, z: 8, core: 2. Of those that a mesh axis runs over, the one named last changes fastest.
Arguments:
- query_mr: bfloat16 [4096, 8192], P('seq', 'chan'), may hold values from -6 to 6
- key_mr: bfloat16 [4096, 8192], P('seq', 'chan'), may hold values from -6 to 6
- value_mr: bfloat16 [4096, 8192], P('seq', 'chan'), may hold values from -6 to 6
- query_li: bfloat16 [4096, 8192], P('seq', 'chan'), may hold values from -6 to 6
- key_li: bfloat16 [4096, 8192], P('seq', 'chan'), may hold values from -6 to 6
- cotangent: bfloat16 [4096, 8192], P('seq', 'chan'), may hold values from -40 to 40
- mr_filter: float32 [512, 128], P('chan'), may hold values from -3.535534 to 3.535534
- norm_gain: float32 [8192], P('chan'), may hold values from 0.1 to 1.9
- li_decay: float32 [512, 16], P('chan'), may hold values from 0.00012207031 to 0.03
- li_residue: float32 [512, 16], P('chan'), may hold values from -1 to 1
Outputs:
- out_li: bfloat16 [4096, 8192], P('seq', 'chan')
- grad_query_mr: bfloat16 [4096, 8192], P('seq', 'chan')
- grad_key_mr: bfloat16 [4096, 8192], P('seq', 'chan')
- grad_value_mr: bfloat16 [4096, 8192], P('seq', 'chan')
- grad_query_li: bfloat16 [4096, 8192], P('seq', 'chan')
- grad_key_li: bfloat16 [4096, 8192], P('seq', 'chan')
- grad_gain: float32 [8192], P('chan')
- grad_filter: float32 [512, 128], P('chan')
The draws below stay inside these ranges and needn't reach their ends.
All inputs are finite; a program needn't handle non-finite values.
Results may differ from the reference program's by a relative error of at most 0.025.
Values may be sent and summed in bfloat16 or wider, within the bound.
A program may use at most 128 MiB of HBM per device.

```python
import math
import jax
import jax.numpy as jnp
from jax import lax

D = 8192
G = 512
MR_TAPS = 128
MODES = 16
TOKENS = 4096


def draw_mr_filter(key, part):
    key_base = jax.random.fold_in(key, 11)
    key_spread = jax.random.fold_in(key, 12)
    trend_scale = 3.0 ** (jnp.arange(G, dtype=jnp.float32) / (G - 1))
    spread = jnp.exp(jax.random.uniform(key_spread, (G, 1), jnp.float32, 0.0, math.log(3.3)))
    base_draw = jnp.clip(jax.random.normal(key_base, (G, MR_TAPS), jnp.float32), -4.0, 4.0)
    return base_draw * trend_scale[:, None] * spread / math.sqrt(MR_TAPS)


def draw_cotangent(key, part):
    key_base = jax.random.fold_in(key, 21)
    key_spread = jax.random.fold_in(key, 22)
    trend_scale = 3.0 ** (jnp.arange(TOKENS, dtype=jnp.float32) / (TOKENS - 1))
    spread = jnp.exp(jax.random.uniform(key_spread, (TOKENS, 1), jnp.float32, 0.0, math.log(3.3)))
    base_draw = jnp.clip(jax.random.normal(key_base, (TOKENS, D), jnp.float32), -4.0, 4.0)
    return (base_draw * trend_scale[:, None] * spread).astype(jnp.bfloat16)


def shard_levels(own_key, dims, shards, least, top_value):
    level, own = 1.0, jax.random.fold_in(own_key, 6)
    for position, blocks in shards:
        draws = jnp.exp(jax.random.uniform(jax.random.fold_in(own, position), (blocks,), jnp.float32, least / len(shards), top_value / len(shards)))
        level = level * jnp.repeat(draws, dims[position] // blocks).reshape([-1 if axis == position else 1 for axis in range(len(dims))])
    return level


def normal_values(key, dims, width, most, cuts=(), kind=jnp.bfloat16):
    level = shard_levels(key, dims, cuts, -0.22, 0.18) if cuts else 1.0
    values = jax.random.normal(key, dims, jnp.float32) * width * level
    return jnp.minimum(jnp.maximum(values, -most), most).astype(kind)


def setup_inputs(seed: int = 0) -> dict:
    keys = jax.random.split(jax.random.key(seed), 11)
    return {
        "query_mr": normal_values(keys[0], (TOKENS, D), 1.0, 6.0, ((0, 32), (1, 8))),
        "key_mr": normal_values(keys[1], (TOKENS, D), 1.0, 6.0, ((0, 32), (1, 8))),
        "value_mr": normal_values(keys[2], (TOKENS, D), 1.0, 6.0, ((0, 32), (1, 8))),
        "query_li": normal_values(keys[3], (TOKENS, D), 1.0, 6.0, ((0, 32), (1, 8))),
        "key_li": normal_values(keys[4], (TOKENS, D), 1.0, 6.0, ((0, 32), (1, 8))),
        "cotangent": draw_cotangent(jax.random.fold_in(keys[10], 71), 0),
        "mr_filter": draw_mr_filter(jax.random.fold_in(keys[10], 71), 0),
        "norm_gain": jnp.clip(1.0 + 0.18 * jax.random.normal(keys[7], (D,), jnp.float32), 0.1, 1.9),
        "li_decay": jnp.clip(jnp.exp(math.log(0.03) - 5.5043554 * jax.random.uniform(keys[8], (G, MODES), jnp.float32) ** shard_levels(keys[8], (G, MODES), ((0, 8),), -0.2, 0.2)), 0.00012207031, 0.03),
        "li_residue": normal_values(keys[9], (G, MODES), 0.25, 1.0, ((0, 8),), jnp.float32),
    }


def rounded(values):
    return lax.optimization_barrier(values.astype(jnp.bfloat16)).astype(jnp.float32)

def split_blocks(values, block_width):
    return values.reshape(values.shape[0], -1, block_width).transpose(1, 0, 2)

def join_blocks(values):
    return values.transpose(1, 0, 2).reshape(values.shape[1], -1)

def grouped_conv(signal, group_taps, backward):
    seq_len, chan_count = signal.shape
    group_size = chan_count // group_taps.shape[0]
    block_width = math.gcd(chan_count, 512)
    if backward:
        signal = jnp.flip(signal, 0)
    pieces = split_blocks(signal, block_width)
    taps_blocks = group_taps.reshape(chan_count // block_width, block_width // group_size, group_taps.shape[1])
    length = 2 * seq_len

    def convolve(pair):
        piece, piece_taps = pair
        expanded = jnp.repeat(piece_taps, group_size, axis=0)
        spectrum = jnp.fft.rfft(piece, length, axis=0) * jnp.fft.rfft(expanded.T, length, axis=0)
        return jnp.fft.irfft(spectrum, length, axis=0)[:seq_len].astype(jnp.float32)
    result = join_blocks(lax.map(convolve, (pieces, taps_blocks)))
    if backward:
        result = jnp.flip(result, 0)
    return result

def grouped_corr(first, second, group_count, tap_count):
    seq_len, chan_count = first.shape
    group_size = chan_count // group_count
    block_width = math.gcd(chan_count, 512)
    length = 2 * seq_len

    def correlate(pair):
        first_piece, second_piece = pair
        spectrum = jnp.fft.rfft(first_piece, length, axis=0) * jnp.conj(jnp.fft.rfft(second_piece, length, axis=0))
        lagged = jnp.fft.irfft(spectrum, length, axis=0)[:tap_count].astype(jnp.float32)
        return lax.optimization_barrier(jnp.sum(lagged.T.reshape(block_width // group_size, group_size, tap_count), axis=1))
    result = lax.map(correlate, (split_blocks(first, block_width), split_blocks(second, block_width)))
    return result.reshape(group_count, tap_count)

def reference(query_mr, key_mr, value_mr, query_li, key_li, cotangent, mr_filter, norm_gain, li_decay, li_residue):
    seq_len = query_mr.shape[0]
    grad_scale = float(seq_len) ** (-0.5)
    taps_mr = rounded(mr_filter)
    mixed_mr = rounded(key_mr.astype(jnp.float32) * value_mr.astype(jnp.float32))
    conv_mr = grouped_conv(mixed_mr, taps_mr, False)
    out_mr = rounded(query_mr.astype(jnp.float32) * conv_mr)
    squares = lax.optimization_barrier(jnp.sum(out_mr * out_mr, axis=1, keepdims=True))
    inv_rms = lax.rsqrt(squares / D + 1e-06)
    normed = out_mr * inv_rms * norm_gain
    mixed_li = key_li.astype(jnp.float32) * normed
    offsets = jnp.arange(seq_len, dtype=jnp.float32)
    norm_res = li_residue * jnp.sqrt(2.0 * li_decay)
    taps_li = jnp.zeros((li_decay.shape[0], seq_len), jnp.float32)
    for mode_index in range(li_decay.shape[1]):
        taps_li = taps_li + norm_res[:, mode_index:mode_index + 1] * jnp.exp(-li_decay[:, mode_index:mode_index + 1] * offsets)
    conv_li = grouped_conv(mixed_li, taps_li, False)
    out_li = (query_li.astype(jnp.float32) * conv_li).astype(jnp.bfloat16)
    cotan_full = cotangent.astype(jnp.float32)
    grad_query_li = (cotan_full * conv_li).astype(jnp.bfloat16)
    back_li = cotan_full * query_li.astype(jnp.float32)
    grad_mixed_li = grouped_conv(back_li, taps_li, True)
    grad_key_li = (grad_mixed_li * normed).astype(jnp.bfloat16)
    grad_normed = grad_mixed_li * key_li.astype(jnp.float32)
    grad_gain = lax.optimization_barrier(jnp.sum(grad_normed * out_mr * inv_rms, axis=0)) * grad_scale
    weighted = grad_normed * norm_gain
    cross_dots = lax.optimization_barrier(jnp.sum(weighted * out_mr, axis=1, keepdims=True))
    grad_out_mr = inv_rms * weighted - out_mr * inv_rms ** 3 * cross_dots / D
    grad_query_mr = (grad_out_mr * conv_mr).astype(jnp.bfloat16)
    back_mr = rounded(grad_out_mr * query_mr.astype(jnp.float32))
    grad_mixed_mr = grouped_conv(back_mr, taps_mr, True)
    grad_key_mr = (grad_mixed_mr * value_mr.astype(jnp.float32)).astype(jnp.bfloat16)
    grad_value_mr = (grad_mixed_mr * key_mr.astype(jnp.float32)).astype(jnp.bfloat16)
    grad_filter = grouped_corr(back_mr, mixed_mr, mr_filter.shape[0], mr_filter.shape[1]) * grad_scale
    return (out_li, grad_query_mr, grad_key_mr, grad_value_mr, grad_query_li, grad_key_li, grad_gain, grad_filter)
```

```python
import functools

import jax
import jax.numpy as jnp
from jax import lax
from jax.experimental import pallas as pl
from jax.experimental.pallas import tpu as pltpu
from jax.sharding import PartitionSpec as P

MESH = pl.DeviceIdType.MESH
F32 = jnp.float32
BF16 = jnp.bfloat16
B = 128
GS = 16
GT = B // GS


def dot(a, b):
    return jnp.dot(a, b, preferred_element_type=F32)


def split(x):
    hi = x.astype(BF16)
    return hi, (x - hi.astype(F32)).astype(BF16)


def kernel(
    n_seq, n_chan, nt,
    q_mr, k_mr, v_mr, q_li, k_li, cot, filt, gain, decay, resid,
    out_li, g_qmr, g_kmr, g_vmr, g_qli, g_kli, g_gain, g_filt,
    ext, bext, tmf, tmb, tlf, tlb, conv, outm, gml, bli, xli, cli,
    winf, winb, woutf, woutb, taps, rtaps, avec,
    bs_src, bs_dst, be_src, be_dst, fs_src, fs_dst, fe_src, fe_dst,
    pbuf, r_src, r_dst, a_src, a_dst,
    hf_s, hf_r, hb_s, hb_r, bs_s, bs_r, be_s, be_r, fs_s, fs_r, fe_s, fe_r,
    p_s, p_r, r_s, r_r, a_s, a_r,
):
    seq = lax.axis_index("seq")
    chan = lax.axis_index("chan")
    units = 2 * nt
    total = float(n_chan * nt * B)
    scale = float(n_seq * B) ** -0.5
    base_b, base_f, base_r = 0, n_seq - units, 0

    lane = lax.broadcasted_iota(jnp.int32, (B, B), 1)
    row = lax.broadcasted_iota(jnp.int32, (B, B), 0)
    lane_group = lane >> 4
    diag_groups = (row >> 4) == lane_group
    eye = row == lane

    def cols(k):
        return pl.ds(pl.multiple_of(k * B, B), B)

    def tile(ref, k):
        return ref[:, cols(k)].astype(F32)

    def pick(stacked):
        out = stacked[0:B]
        for g in range(1, GT):
            out = jnp.where(lane_group == g, stacked[g * B:(g + 1) * B], out)
        return out

    def squeeze(full):
        return jnp.sum(jnp.where(diag_groups, full, 0.0).reshape(GT, GS, B), axis=0)

    def remote(src, dst, ss, rs, axis, target):
        return pltpu.make_async_remote_copy(
            src_ref=src, dst_ref=dst, send_sem=ss, recv_sem=rs,
            device_id={axis: target}, device_id_type=MESH,
        )

    barrier = pltpu.get_barrier_semaphore()

    @pl.loop(1, n_seq)
    def _(d):
        pl.semaphore_signal(barrier, inc=1, device_id={"seq": lax.rem(seq + d, n_seq)}, device_id_type=MESH)

    @pl.loop(1, n_chan)
    def _(d):
        pl.semaphore_signal(barrier, inc=1, device_id={"chan": lax.rem(chan + d, n_chan)}, device_id_type=MESH)

    @pl.loop(0, nt)
    def _(k):
        ext[k, 0:B, :] = (tile(k_mr, k) * tile(v_mr, k)).astype(BF16)

    pl.semaphore_wait(barrier, n_seq - 1 + n_chan - 1)

    def halo_f(k):
        return remote(ext.at[k, pl.ds(0, B)], ext.at[k, pl.ds(B, B)], hf_s.at[k], hf_r.at[k], "seq", lax.rem(seq + 1, n_seq))

    def halo_b(k):
        return remote(bext.at[k, pl.ds(0, B)], bext.at[k, pl.ds(B, B)], hb_s.at[k], hb_r.at[k], "seq",
                      lax.rem(seq + n_seq - 1, n_seq))

    @pl.when(seq < n_seq - 1)
    def _():
        @pl.loop(0, nt)
        def _(k):
            halo_f(k).start()

    @pl.when(seq == 0)
    def _():
        @pl.loop(0, nt)
        def _(k):
            ext[k, B:2 * B, :] = jnp.zeros((B, B), BF16)

    @pl.when(seq == n_seq - 1)
    def _():
        @pl.loop(0, nt)
        def _(k):
            bext[k, B:2 * B, :] = jnp.zeros((B, B), BF16)

    def scatter_copy(src, dst, ss, rs, base, u):
        return remote(src.at[u], dst.at[seq], ss.at[u], rs.at[seq], "seq", base + u)

    def scatter(src, dst, ss, rs, base, count):
        for u in range(count):
            @pl.when(seq != base + u)
            def _():
                scatter_copy(src, dst, ss, rs, base, u).start()

            @pl.when(seq == base + u)
            def _():
                dst[seq] = src[u]

    def scatter_wait(src, dst, ss, rs, base, count):
        for u in range(count):
            @pl.when(seq != base + u)
            def _():
                scatter_copy(src, dst, ss, rs, base, u).wait_send()

    def owner_wait(src, dst, ss, rs):
        @pl.loop(1, n_seq)
        def _(d):
            other = lax.rem(seq + d, n_seq)
            remote(src.at[0], dst.at[other], ss.at[0], rs.at[other], "seq", other).wait_recv()

    def answer_wait(src, dst, ss, rs, base, count):
        for u in range(count):
            @pl.when(seq != base + u)
            def _():
                remote(src.at[0], dst.at[u], ss.at[0], rs.at[u], "seq", base + u).wait_recv()

    def owns(base, count):
        return jnp.logical_and(seq >= base, seq < base + count)

    def owner_scan(src, dst, ss, rs, e_src, e_dst, es, er, base, backward):
        @pl.when(owns(base, units))
        def _():
            owner_wait(src, dst, ss, rs)
            u = seq - base
            fade = avec[u]

            def step(i, state):
                q = n_seq - 1 - i if backward else i
                e_src[q] = state
                return fade * state + dst[q]

            lax.fori_loop(0, n_seq, step, jnp.zeros((8, B), F32))
            e_dst[u] = e_src[seq]

            @pl.loop(1, n_seq)
            def _(d):
                other = lax.rem(seq + d, n_seq)
                remote(e_src.at[other], e_dst.at[u], es.at[other], er.at[u], "seq", other).start()

    def owner_sends_wait(e_src, e_dst, es, er, base, count, one):
        @pl.when(owns(base, count))
        def _():
            u = seq - base

            @pl.loop(1, n_seq)
            def _(d):
                other = lax.rem(seq + d, n_seq)
                src = e_src.at[0] if one else e_src.at[other]
                remote(src, e_dst.at[u], es.at[other], er.at[u], "seq", other).wait_send()

    eye_modes = lax.broadcasted_iota(jnp.int32, (GS, GS), 0) == lax.broadcasted_iota(jnp.int32, (GS, GS), 1)
    time = lane.astype(F32)

    @pl.loop(0, nt)
    def _(k):
        def column(ref):
            parts = []
            for g in range(GT):
                values = ref[pl.ds(k * GT + g, 1), :]
                parts.append(jnp.sum(jnp.where(eye_modes, values, 0.0), axis=1, keepdims=True))
            return jnp.concatenate(parts, axis=0)

        rate = column(decay)
        weight = column(resid) * jnp.sqrt(2.0 * rate)
        fading = jnp.exp(-rate * time)
        hi, lo = split(fading)
        winb[k, 0:B, :] = hi
        winb[k, B:2 * B, :] = lo
        back = (tile(cot, k) * tile(q_li, k)).astype(BF16)
        bli[k] = back
        states = squeeze(dot(hi, back) + dot(lo, back))
        bs_src[2 * k] = states[0:8]
        bs_src[2 * k + 1] = states[8:16]
        powers = squeeze(jnp.broadcast_to(jnp.exp(-rate * float(B)), (B, B)))
        avec[2 * k] = powers[0:8]
        avec[2 * k + 1] = powers[8:16]
        taps[1, pl.ds(pl.multiple_of(k * GT, GT), GT), :] = jnp.sum((weight * fading).reshape(GT, GS, B), axis=1)
        hi, lo = split(jnp.exp(-rate * (B - 1.0 - time)))
        winf[k, 0:B, :] = hi
        winf[k, B:2 * B, :] = lo
        hi, lo = split((weight * jnp.exp(-rate * (B - time))).T)
        woutb[k, :, 0:B] = hi
        woutb[k, :, B:2 * B] = lo
        hi, lo = split((weight * jnp.exp(-rate * (time + 1.0))).T)
        woutf[k, :, 0:B] = hi
        woutf[k, :, B:2 * B] = lo

    scatter(bs_src, bs_dst, bs_s, bs_r, base_b, units)

    reflect = jnp.where(row == ((B - lane) & (B - 1)), 1.0, 0.0)
    taps[0] = filt[...].astype(BF16).astype(F32)
    for which in range(2):
        rtaps[which] = dot(taps[which].astype(BF16), reflect.astype(BF16))

    def rolled(ref, which, group):
        line = jnp.broadcast_to(ref[which, pl.ds(group, 1), :], (B, B))
        return pltpu.roll(line, 0, axis=1, stride=1, stride_axis=0)

    def build(ref, which, mask, out):
        @pl.loop(0, nt)
        def _(k):
            for g in range(GT):
                matrix = rolled(ref, which, k * GT + g)
                out[k, g * B:(g + 1) * B, 0:B] = jnp.where(mask, matrix, 0.0).astype(BF16)
                if which == 0:
                    out[k, g * B:(g + 1) * B, B:2 * B] = jnp.where(mask, 0.0, matrix).astype(BF16)

    build(rtaps, 0, lane <= row, tmf)
    build(taps, 1, lane >= row, tlb)

    owner_scan(bs_src, bs_dst, bs_s, bs_r, be_src, be_dst, be_s, be_r, base_b, True)

    def carried(wout, e_dst, k):
        state = jnp.concatenate([e_dst[2 * k], e_dst[2 * k + 1]], axis=0)
        hi, lo = split(jnp.where(diag_groups, jnp.concatenate([state] * GT, axis=0), 0.0))
        return dot(wout[k], jnp.concatenate([hi, hi], axis=0)) + dot(wout[k, :, 0:B], lo)

    @pl.loop(0, nt)
    def _(k):
        gml[k] = pick(dot(tlb[k], bli[k]))

    squares = jnp.zeros((B, B), F32)

    def mr_step(k, squares):
        @pl.when(seq > 0)
        def _():
            halo_f(k).wait_recv()

        value = pick(dot(tmf[k], ext[k]))
        conv[k] = value
        gated = (tile(q_mr, k) * value).astype(BF16).astype(F32)
        outm[k] = gated
        return squares + gated * gated

    squares = lax.fori_loop(0, nt, mr_step, squares)

    answer_wait(be_src, be_dst, be_s, be_r, base_b, units)

    def li_step(k, cross):
        grad = gml[k] + carried(woutb, be_dst, k)
        gml[k] = grad
        return cross + grad * tile(k_li, k) * outm[k] * gain[pl.ds(k, 1), :]

    cross = lax.fori_loop(0, nt, li_step, jnp.zeros((B, B), F32))

    def as_row(partial):
        column = jnp.sum(partial, axis=1, keepdims=True)
        return jnp.sum(jnp.where(eye, column, 0.0), axis=0, keepdims=True)

    def as_column(line):
        return jnp.sum(jnp.where(eye, line, 0.0), axis=1, keepdims=True)

    row8 = lax.broadcasted_iota(jnp.int32, (8, B), 0)
    pbuf[chan] = jnp.where(row8 == 0, as_row(squares), as_row(cross))

    def psum_copy(d):
        other = lax.rem(chan + d, n_chan)
        return remote(pbuf.at[chan], pbuf.at[chan], p_s.at[other], p_r.at[chan], "chan", other)

    @pl.loop(1, n_chan)
    def _(d):
        psum_copy(d).start()

    build(taps, 0, lane >= row, tmb)
    build(rtaps, 1, lane <= row, tlf)

    @pl.loop(1, n_chan)
    def _(d):
        other = lax.rem(chan + d, n_chan)
        remote(pbuf.at[other], pbuf.at[other], p_s.at[other], p_r.at[other], "chan", other).wait_recv()

    sums = pbuf[0]
    for c in range(1, n_chan):
        sums = sums + pbuf[c]
    inv_row = lax.rsqrt(sums[0:1] / total + 1e-06)
    inv = as_column(inv_row)
    pull = as_column(inv_row * inv_row * inv_row * sums[1:2] / total)

    @pl.loop(0, nt)
    def _(k):
        gated, grad, key = outm[k], gml[k], tile(k_li, k)
        gains = gain[pl.ds(k, 1), :]
        scaled = gated * inv
        normed = scaled * gains
        grad_normed = grad * key
        g_kli[:, cols(k)] = (grad * normed).astype(BF16)
        grad_out = inv * (grad_normed * gains) - gated * pull
        bext[k, 0:B, :] = (grad_out * tile(q_mr, k)).astype(BF16)

        @pl.when(seq > 0)
        def _():
            halo_b(k).start()

        g_qmr[:, cols(k)] = (grad_out * conv[k]).astype(BF16)
        r_src[nt, pl.ds(k, 1), :] = jnp.sum(grad_normed * scaled, axis=0, keepdims=True)
        mixed = (key * normed).astype(BF16)
        xli[k] = mixed
        both = dot(winf[k], mixed)
        states = squeeze(both[0:B] + both[B:2 * B])
        fs_src[2 * k] = states[0:8]
        fs_src[2 * k + 1] = states[8:16]

    if nt < 8:
        r_src[nt, nt:8, :] = jnp.zeros((8 - nt, B), F32)
    scatter(fs_src, fs_dst, fs_s, fs_r, base_f, units)

    row64 = lax.broadcasted_iota(jnp.int32, (8 * GT, B), 0)

    @pl.loop(0, nt)
    def _(k):
        back = bext[k, 0:B, :]
        masked = jnp.concatenate([jnp.where(lane_group == g, back, jnp.zeros_like(back)) for g in range(GT)], axis=0)
        gram = lax.dot_general(masked, ext[k], (((1,), (1,)), ((), ())), preferred_element_type=F32)
        sums = []
        for g in range(GT):
            rows = gram[g * B:(g + 1) * B]
            cyclic = jnp.where(lane <= row, rows[:, 0:B], rows[:, B:2 * B])
            acc = cyclic[B - 8:B]
            for b in range(B // 8 - 2, -1, -1):
                acc = pltpu.roll(acc, B - 8, axis=1) + cyclic[8 * b:8 * b + 8]
            sums.append(acc)
        acc = jnp.concatenate(sums, axis=0)
        for bit in range(3):
            acc = jnp.where(((row64 >> bit) & 1) == 1, pltpu.roll(acc, B - (1 << bit), axis=1), acc)
        diagonals = jnp.sum(acc.reshape(GT, 8, B), axis=1)
        hi = diagonals.astype(BF16)
        rest = diagonals - hi.astype(F32)
        mid, lo = split(rest)
        parts = dot(jnp.concatenate([hi.astype(F32), mid.astype(F32), lo.astype(F32)], axis=0).astype(BF16),
                    reflect.astype(BF16))
        r_src[k] = parts[0:8] + parts[8:16] + parts[16:24]

    scatter(r_src, r_dst, r_s, r_r, base_r, nt + 1)

    owner_scan(fs_src, fs_dst, fs_s, fs_r, fe_src, fe_dst, fe_s, fe_r, base_f, False)

    @pl.loop(0, nt)
    def _(k):
        cli[k] = pick(dot(tlf[k], xli[k]))

    @pl.when(owns(base_r, nt + 1))
    def _():
        owner_wait(r_src, r_dst, r_s, r_r)
        u = seq - base_r
        result = lax.fori_loop(1, n_seq, lambda q, acc: acc + r_dst[q], r_dst[0]) * scale
        a_src[0] = result
        a_dst[u] = result

        @pl.loop(1, n_seq)
        def _(d):
            other = lax.rem(seq + d, n_seq)
            remote(a_src.at[0], a_dst.at[u], a_s.at[other], a_r.at[u], "seq", other).start()

    answer_wait(fe_src, fe_dst, fe_s, fe_r, base_f, units)

    @pl.loop(0, nt)
    def _(k):
        value = cli[k] + carried(woutf, fe_dst, k)
        out_li[:, cols(k)] = (tile(q_li, k) * value).astype(BF16)
        g_qli[:, cols(k)] = (tile(cot, k) * value).astype(BF16)

    @pl.loop(0, nt)
    def _(k):
        @pl.when(seq < n_seq - 1)
        def _():
            halo_b(k).wait_recv()

        grad = pick(dot(tmb[k], bext[k]))
        g_kmr[:, cols(k)] = (grad * tile(v_mr, k)).astype(BF16)
        g_vmr[:, cols(k)] = (grad * tile(k_mr, k)).astype(BF16)

    answer_wait(a_src, a_dst, a_s, a_r, base_r, nt + 1)
    for k in range(nt):
        g_filt[k * 8:(k + 1) * 8, :] = a_dst[k]
    g_gain[...] = a_dst[nt, 0:nt, :]

    @pl.when(seq < n_seq - 1)
    def _():
        @pl.loop(0, nt)
        def _(k):
            halo_f(k).wait_send()

    @pl.when(seq > 0)
    def _():
        @pl.loop(0, nt)
        def _(k):
            halo_b(k).wait_send()

    scatter_wait(bs_src, bs_dst, bs_s, bs_r, base_b, units)
    scatter_wait(fs_src, fs_dst, fs_s, fs_r, base_f, units)
    scatter_wait(r_src, r_dst, r_s, r_r, base_r, nt + 1)
    owner_sends_wait(be_src, be_dst, be_s, be_r, base_b, units, False)
    owner_sends_wait(fe_src, fe_dst, fe_s, fe_r, base_f, units, False)
    owner_sends_wait(a_src, a_dst, a_s, a_r, base_r, nt + 1, True)

    @pl.loop(1, n_chan)
    def _(d):
        psum_copy(d).wait_send()


def solution(mesh):
    n_seq, n_chan = mesh.shape["seq"], mesh.shape["chan"]

    def on_device(q_mr, k_mr, v_mr, q_li, k_li, cot, filt, gain, decay, resid):
        rows, width = q_mr.shape
        nt = width // B
        units = 2 * nt
        wide = jax.ShapeDtypeStruct((rows, width), BF16)
        vmem = pl.BlockSpec(memory_space=pltpu.VMEM)
        dma = pltpu.SemaphoreType.DMA
        state = lambda count: pltpu.VMEM((count, 8, B), F32)
        plane = lambda kind: pltpu.VMEM((nt, B, B), kind)
        outs = pl.pallas_call(
            functools.partial(kernel, n_seq, n_chan, nt),
            out_shape=[wide] * 6 + [jax.ShapeDtypeStruct((nt, B), F32), jax.ShapeDtypeStruct(filt.shape, F32)],
            in_specs=[vmem] * 10,
            out_specs=[vmem] * 8,
            scratch_shapes=[
                pltpu.VMEM((nt, 2 * B, B), BF16), pltpu.VMEM((nt, 2 * B, B), BF16),
                pltpu.VMEM((nt, GT * B, 2 * B), BF16), pltpu.VMEM((nt, GT * B, 2 * B), BF16),
                pltpu.VMEM((nt, GT * B, B), BF16), pltpu.VMEM((nt, GT * B, B), BF16),
                plane(F32), plane(F32), plane(F32), plane(BF16), plane(BF16), plane(F32),
                pltpu.VMEM((nt, 2 * B, B), BF16), pltpu.VMEM((nt, 2 * B, B), BF16),
                pltpu.VMEM((nt, B, 2 * B), BF16), pltpu.VMEM((nt, B, 2 * B), BF16),
                pltpu.VMEM((2, nt * GT, B), F32), pltpu.VMEM((2, nt * GT, B), F32), state(units),
                state(units), state(n_seq), state(n_seq), state(units),
                state(units), state(n_seq), state(n_seq), state(units),
                state(n_chan), state(nt + 1), state(n_seq), state(1), state(nt + 1),
                dma((nt,)), dma((nt,)), dma((nt,)), dma((nt,)),
                dma((units,)), dma((n_seq,)), dma((n_seq,)), dma((units,)),
                dma((units,)), dma((n_seq,)), dma((n_seq,)), dma((units,)),
                dma((n_chan,)), dma((n_chan,)),
                dma((nt + 1,)), dma((n_seq,)), dma((n_seq,)), dma((nt + 1,)),
            ],
            compiler_params=pltpu.CompilerParams(
                collective_id=0, has_side_effects=True, vmem_limit_bytes=48 * 1024 * 1024
            ),
        )(q_mr, k_mr, v_mr, q_li, k_li, cot, filt, gain.reshape(nt, B), decay, resid)
        return (*outs[:6], outs[6].reshape(width), outs[7])

    wide, by_group, by_chan = P("seq", "chan"), P("chan", None), P("chan")
    return jax.shard_map(
        on_device, mesh=mesh,
        in_specs=(wide,) * 6 + (by_group, by_chan, by_group, by_group),
        out_specs=(wide,) * 6 + (by_chan, by_group),
        check_vma=False,
    )
```

```python
import functools

import jax
import jax.numpy as jnp
from jax import lax
from jax.experimental import pallas as pl
from jax.experimental.pallas import tpu as pltpu
from jax.sharding import PartitionSpec as P

MESH = pl.DeviceIdType.MESH
F32 = jnp.float32
BF16 = jnp.bfloat16
B = 128
GS = 16
GT = B // GS


def dot(a, b):
    return jnp.dot(a, b, preferred_element_type=F32)


def split(x):
    hi = x.astype(BF16)
    return hi, (x - hi.astype(F32)).astype(BF16)


def kernel(
    n_seq, n_chan, nt,
    q_mr_in, k_mr_in, v_mr_in, q_li_in, k_li_in, cot_in, filt_in, gain_in, decay_in, resid_in,
    out_li, g_qmr, g_kmr, g_vmr, g_qli, g_kli, g_gain, g_filt,
    q_mr, k_mr, v_mr, q_li, k_li, cot, filt, gain, decay, resid,
    ext, bext, tmf, tmb, tlf, tlb, conv, outm, gml, bli, xli, cli,
    winf, winb, woutf, woutb, taps, rtaps, avec,
    bs_src, bs_dst, be_src, be_dst, fs_src, fs_dst, fe_src, fe_dst,
    pbuf, r_src, r_dst, a_src, a_dst,
    in_sem, hf_s, hf_r, hb_s, hb_r, bs_s, bs_r, be_s, be_r, fs_s, fs_r, fe_s, fe_r,
    p_s, p_r, r_s, r_r, a_s, a_r,
):
    seq = lax.axis_index("seq")
    chan = lax.axis_index("chan")
    units = 2 * nt
    total = float(n_chan * nt * B)
    scale = float(n_seq * B) ** -0.5
    base_b, base_f, base_r = 0, n_seq - units, 0

    lane = lax.broadcasted_iota(jnp.int32, (B, B), 1)
    row = lax.broadcasted_iota(jnp.int32, (B, B), 0)
    lane_group = lane >> 4
    diag_groups = (row >> 4) == lane_group
    eye = row == lane

    def cols(k):
        return pl.ds(pl.multiple_of(k * B, B), B)

    def tile(ref, k):
        return ref[:, cols(k)].astype(F32)

    def pick(stacked):
        out = stacked[0:B]
        for g in range(1, GT):
            out = jnp.where(lane_group == g, stacked[g * B:(g + 1) * B], out)
        return out

    def squeeze(full):
        return jnp.sum(jnp.where(diag_groups, full, 0.0).reshape(GT, GS, B), axis=0)

    def remote(src, dst, ss, rs, axis, target):
        return pltpu.make_async_remote_copy(
            src_ref=src, dst_ref=dst, send_sem=ss, recv_sem=rs,
            device_id={axis: target}, device_id_type=MESH,
        )

    fetched = (k_mr, v_mr, decay, resid, cot, q_li, filt, gain, q_mr, k_li)
    fetches = [
        pltpu.make_async_copy(src, dst, in_sem.at[i])
        for i, (src, dst) in enumerate(zip(
            (k_mr_in, v_mr_in, decay_in, resid_in, cot_in, q_li_in, filt_in, gain_in, q_mr_in, k_li_in), fetched))
    ]
    for fetch in fetches:
        fetch.start()
    barrier = pltpu.get_barrier_semaphore()

    @pl.loop(1, n_seq)
    def _(d):
        pl.semaphore_signal(barrier, inc=1, device_id={"seq": lax.rem(seq + d, n_seq)}, device_id_type=MESH)

    @pl.loop(1, n_chan)
    def _(d):
        pl.semaphore_signal(barrier, inc=1, device_id={"chan": lax.rem(chan + d, n_chan)}, device_id_type=MESH)

    fetches[0].wait()
    fetches[1].wait()

    @pl.loop(0, nt)
    def _(k):
        ext[k, 0:B, :] = (tile(k_mr, k) * tile(v_mr, k)).astype(BF16)

    pl.semaphore_wait(barrier, n_seq - 1 + n_chan - 1)

    def halo_f(k):
        return remote(ext.at[k, pl.ds(0, B)], ext.at[k, pl.ds(B, B)], hf_s, hf_r.at[k], "seq", lax.rem(seq + 1, n_seq))

    def halo_b(k):
        return remote(bext.at[k, pl.ds(0, B)], bext.at[k, pl.ds(B, B)], hb_s, hb_r.at[k], "seq",
                      lax.rem(seq + n_seq - 1, n_seq))

    @pl.when(seq < n_seq - 1)
    def _():
        @pl.loop(0, nt)
        def _(k):
            halo_f(k).start()

    @pl.when(seq == 0)
    def _():
        @pl.loop(0, nt)
        def _(k):
            ext[k, B:2 * B, :] = jnp.zeros((B, B), BF16)

    @pl.when(seq == n_seq - 1)
    def _():
        @pl.loop(0, nt)
        def _(k):
            bext[k, B:2 * B, :] = jnp.zeros((B, B), BF16)

    def owns(base, count):
        return jnp.logical_and(seq >= base, seq < base + count)

    def scatter(src, dst, ss, rs, base, count):
        for u in range(count):
            @pl.when(seq != base + u)
            def _():
                remote(src.at[u], dst.at[seq], ss, rs, "seq", base + u).start()

            @pl.when(seq == base + u)
            def _():
                dst[seq] = src[u]

    def answer(e_src, e_dst, es, er, u, one):
        @pl.loop(1, n_seq)
        def _(d):
            other = lax.rem(seq + d, n_seq)
            remote(e_src.at[0] if one else e_src.at[other], e_dst.at[u], es, er, "seq", other).start()

    def several(ref, ss, rs, count):
        return remote(ref.at[pl.ds(0, count)], ref.at[pl.ds(0, count)], ss, rs, "seq", lax.rem(seq + 1, n_seq))

    def but_own(base, count, wait):
        @pl.when(owns(base, count))
        def _():
            wait(count - 1)

        @pl.when(jnp.logical_not(owns(base, count)))
        def _():
            wait(count)

    def scatter_wait(src, ss, rs, base, count):
        but_own(base, count, lambda n: several(src, ss, rs, n).wait_send())

    def answer_wait(e_dst, es, er, base, count):
        but_own(base, count, lambda n: several(e_dst, es, er, n).wait_recv())

    def owner_wait(dst, ss, rs):
        several(dst, ss, rs, n_seq - 1).wait_recv()

    def owner_scan(dst, ss, rs, e_src, e_dst, es, er, base, backward):
        @pl.when(owns(base, units))
        def _():
            owner_wait(dst, ss, rs)
            u = seq - base
            fade = avec[u]

            def step(i, state):
                q = n_seq - 1 - i if backward else i
                e_src[q] = state
                return fade * state + dst[q]

            lax.fori_loop(0, n_seq, step, jnp.zeros((8, B), F32))
            e_dst[u] = e_src[seq]
            answer(e_src, e_dst, es, er, u, False)

    group_lane = lax.broadcasted_iota(jnp.int32, decay.shape, 1)
    for fetch in fetches[2:6]:
        fetch.wait()
    time = lane.astype(F32)

    @pl.loop(0, nt)
    def _(k):
        def column(values):
            return jnp.concatenate([
                jnp.sum(jnp.where(group_lane == k * GT + g, values, 0.0), axis=1, keepdims=True) for g in range(GT)
            ], axis=0)

        rate = column(decay[...])
        weight = column(resid[...]) * jnp.sqrt(2.0 * rate)
        fading = jnp.exp(-rate * time)
        hi, lo = split(fading)
        winb[k, 0:B, :] = hi
        winb[k, B:2 * B, :] = lo
        back = (tile(cot, k) * tile(q_li, k)).astype(BF16)
        bli[k] = back
        states = squeeze(dot(hi, back) + dot(lo, back))
        bs_src[2 * k] = states[0:8]
        bs_src[2 * k + 1] = states[8:16]
        powers = squeeze(jnp.broadcast_to(jnp.exp(-rate * float(B)), (B, B)))
        avec[2 * k] = powers[0:8]
        avec[2 * k + 1] = powers[8:16]
        taps[1, pl.ds(pl.multiple_of(k * GT, GT), GT), :] = jnp.sum((weight * fading).reshape(GT, GS, B), axis=1)
        hi, lo = split(jnp.exp(-rate * (B - 1.0 - time)))
        winf[k, 0:B, :] = hi
        winf[k, B:2 * B, :] = lo
        hi, lo = split((weight * jnp.exp(-rate * (B - time))).T)
        woutb[k, :, 0:B] = hi
        woutb[k, :, B:2 * B] = lo
        hi, lo = split((weight * jnp.exp(-rate * (time + 1.0))).T)
        woutf[k, :, 0:B] = hi
        woutf[k, :, B:2 * B] = lo

    scatter(bs_src, bs_dst, bs_s, bs_r, base_b, units)

    for fetch in fetches[6:]:
        fetch.wait()
    reflect = jnp.where(row == ((B - lane) & (B - 1)), 1.0, 0.0)
    taps[0] = filt[...].astype(BF16).astype(F32)
    for which in range(2):
        rtaps[which] = dot(taps[which].astype(BF16), reflect.astype(BF16))

    def rolled(ref, which, group):
        line = jnp.broadcast_to(ref[which, pl.ds(group, 1), :], (B, B))
        return pltpu.roll(line, 0, axis=1, stride=1, stride_axis=0)

    def build(ref, which, mask, out):
        @pl.loop(0, nt)
        def _(k):
            for g in range(GT):
                matrix = rolled(ref, which, k * GT + g)
                out[k, g * B:(g + 1) * B, 0:B] = jnp.where(mask, matrix, 0.0).astype(BF16)
                if which == 0:
                    out[k, g * B:(g + 1) * B, B:2 * B] = jnp.where(mask, 0.0, matrix).astype(BF16)

    build(rtaps, 0, lane <= row, tmf)
    build(taps, 1, lane >= row, tlb)

    owner_scan(bs_dst, bs_s, bs_r, be_src, be_dst, be_s, be_r, base_b, True)

    def carried(wout, e_dst, k):
        state = jnp.concatenate([e_dst[2 * k], e_dst[2 * k + 1]], axis=0)
        hi, lo = split(jnp.where(diag_groups, jnp.concatenate([state] * GT, axis=0), 0.0))
        return dot(wout[k], jnp.concatenate([hi, hi], axis=0)) + dot(wout[k, :, 0:B], lo)

    @pl.loop(0, nt)
    def _(k):
        gml[k] = pick(dot(tlb[k], bli[k]))

    squares = jnp.zeros((B, B), F32)

    def mr_step(k, squares):
        @pl.when(seq > 0)
        def _():
            halo_f(k).wait_recv()

        value = pick(dot(tmf[k], ext[k]))
        conv[k] = value
        gated = (tile(q_mr, k) * value).astype(BF16).astype(F32)
        outm[k] = gated
        return squares + gated * gated

    squares = lax.fori_loop(0, nt, mr_step, squares)

    answer_wait(be_dst, be_s, be_r, base_b, units)

    def li_step(k, cross):
        grad = gml[k] + carried(woutb, be_dst, k)
        gml[k] = grad
        return cross + grad * tile(k_li, k) * outm[k] * gain[pl.ds(k, 1), :]

    cross = lax.fori_loop(0, nt, li_step, jnp.zeros((B, B), F32))

    def as_row(partial):
        column = jnp.sum(partial, axis=1, keepdims=True)
        return jnp.sum(jnp.where(eye, column, 0.0), axis=0, keepdims=True)

    def as_column(line):
        return jnp.sum(jnp.where(eye, line, 0.0), axis=1, keepdims=True)

    row8 = lax.broadcasted_iota(jnp.int32, (8, B), 0)
    pbuf[chan] = jnp.where(row8 == 0, as_row(squares), as_row(cross))

    def psum_copy(d):
        other = lax.rem(chan + d, n_chan)
        return remote(pbuf.at[chan], pbuf.at[chan], p_s, p_r, "chan", other)

    @pl.loop(1, n_chan)
    def _(d):
        psum_copy(d).start()

    build(taps, 0, lane >= row, tmb)
    build(rtaps, 1, lane <= row, tlf)

    psum_all = remote(pbuf.at[pl.ds(0, n_chan - 1)], pbuf.at[pl.ds(0, n_chan - 1)], p_s, p_r, "chan",
                      lax.rem(chan + 1, n_chan))
    psum_all.wait_recv()

    sums = pbuf[0]
    for c in range(1, n_chan):
        sums = sums + pbuf[c]
    inv_row = lax.rsqrt(sums[0:1] / total + 1e-06)
    inv = as_column(inv_row)
    pull = as_column(inv_row * inv_row * inv_row * sums[1:2] / total)

    @pl.loop(0, nt)
    def _(k):
        gated, grad, key = outm[k], gml[k], tile(k_li, k)
        gains = gain[pl.ds(k, 1), :]
        scaled = gated * inv
        normed = scaled * gains
        grad_normed = grad * key
        g_kli[:, cols(k)] = (grad * normed).astype(BF16)
        grad_out = inv * (grad_normed * gains) - gated * pull
        bext[k, 0:B, :] = (grad_out * tile(q_mr, k)).astype(BF16)

        @pl.when(seq > 0)
        def _():
            halo_b(k).start()

        g_qmr[:, cols(k)] = (grad_out * conv[k]).astype(BF16)
        r_src[nt, pl.ds(k, 1), :] = jnp.sum(grad_normed * scaled, axis=0, keepdims=True)
        mixed = (key * normed).astype(BF16)
        xli[k] = mixed
        both = dot(winf[k], mixed)
        states = squeeze(both[0:B] + both[B:2 * B])
        fs_src[2 * k] = states[0:8]
        fs_src[2 * k + 1] = states[8:16]

    if nt < 8:
        r_src[nt, nt:8, :] = jnp.zeros((8 - nt, B), F32)
    scatter(fs_src, fs_dst, fs_s, fs_r, base_f, units)

    row64 = lax.broadcasted_iota(jnp.int32, (8 * GT, B), 0)

    @pl.loop(0, nt)
    def _(k):
        back = bext[k, 0:B, :]
        masked = jnp.concatenate([jnp.where(lane_group == g, back, jnp.zeros_like(back)) for g in range(GT)], axis=0)
        gram = lax.dot_general(masked, ext[k], (((1,), (1,)), ((), ())), preferred_element_type=F32)
        sums = []
        for g in range(GT):
            rows = gram[g * B:(g + 1) * B]
            cyclic = jnp.where(lane <= row, rows[:, 0:B], rows[:, B:2 * B])
            half = B // 2
            while half >= 8:
                cyclic = cyclic[0:half] + pltpu.roll(cyclic[half:2 * half], B - half, axis=1)
                half //= 2
            sums.append(cyclic)
        acc = jnp.concatenate(sums, axis=0)
        for bit in range(3):
            acc = jnp.where(((row64 >> bit) & 1) == 1, pltpu.roll(acc, B - (1 << bit), axis=1), acc)
        diagonals = jnp.sum(acc.reshape(GT, 8, B), axis=1)
        hi = diagonals.astype(BF16)
        rest = diagonals - hi.astype(F32)
        mid, lo = split(rest)
        parts = dot(jnp.concatenate([hi.astype(F32), mid.astype(F32), lo.astype(F32)], axis=0).astype(BF16),
                    reflect.astype(BF16))
        r_src[k] = parts[0:8] + parts[8:16] + parts[16:24]

    scatter(r_src, r_dst, r_s, r_r, base_r, nt + 1)

    owner_scan(fs_dst, fs_s, fs_r, fe_src, fe_dst, fe_s, fe_r, base_f, False)

    @pl.loop(0, nt)
    def _(k):
        cli[k] = pick(dot(tlf[k], xli[k]))

    @pl.when(owns(base_r, nt + 1))
    def _():
        owner_wait(r_dst, r_s, r_r)
        u = seq - base_r
        result = lax.fori_loop(1, n_seq, lambda q, acc: acc + r_dst[q], r_dst[0]) * scale
        a_src[0] = result
        a_dst[u] = result
        answer(a_src, a_dst, a_s, a_r, u, True)

    answer_wait(fe_dst, fe_s, fe_r, base_f, units)

    @pl.loop(0, nt)
    def _(k):
        value = cli[k] + carried(woutf, fe_dst, k)
        out_li[:, cols(k)] = (tile(q_li, k) * value).astype(BF16)
        g_qli[:, cols(k)] = (tile(cot, k) * value).astype(BF16)

    @pl.loop(0, nt)
    def _(k):
        @pl.when(seq < n_seq - 1)
        def _():
            halo_b(k).wait_recv()

        grad = pick(dot(tmb[k], bext[k]))
        g_kmr[:, cols(k)] = (grad * tile(v_mr, k)).astype(BF16)
        g_vmr[:, cols(k)] = (grad * tile(k_mr, k)).astype(BF16)

    answer_wait(a_dst, a_s, a_r, base_r, nt + 1)
    for k in range(nt):
        g_filt[k * 8:(k + 1) * 8, :] = a_dst[k]
    g_gain[...] = a_dst[nt, 0:nt, :]

    @pl.when(seq < n_seq - 1)
    def _():
        remote(ext.at[:, pl.ds(0, B)], ext.at[:, pl.ds(B, B)], hf_s, hf_r.at[0], "seq", lax.rem(seq + 1, n_seq)).wait_send()

    @pl.when(seq > 0)
    def _():
        remote(bext.at[:, pl.ds(0, B)], bext.at[:, pl.ds(B, B)], hb_s, hb_r.at[0], "seq",
               lax.rem(seq + n_seq - 1, n_seq)).wait_send()

    scatter_wait(bs_src, bs_s, bs_r, base_b, units)
    scatter_wait(fs_src, fs_s, fs_r, base_f, units)
    scatter_wait(r_src, r_s, r_r, base_r, nt + 1)
    for e_src, es, er, base in ((be_src, be_s, be_r, base_b), (fe_src, fe_s, fe_r, base_f)):
        @pl.when(owns(base, units))
        def _():
            several(e_src, es, er, n_seq - 1).wait_send()

    @pl.when(owns(base_r, nt + 1))
    def _():
        several(r_dst, a_s, a_r, n_seq - 1).wait_send()

    psum_all.wait_send()


def deliver(*refs):
    count = len(refs) // 2
    sem = refs[-1]
    copies = [pltpu.make_async_copy(refs[i], refs[count + i], sem.at[i]) for i in range(count)]
    for copy in copies:
        copy.start()
    for copy in copies:
        copy.wait()


def solution(mesh):
    n_seq, n_chan = mesh.shape["seq"], mesh.shape["chan"]

    def on_device(q_mr, k_mr, v_mr, q_li, k_li, cot, filt, gain, decay, resid):
        rows, width = q_mr.shape
        nt = width // B
        units = 2 * nt
        groups, taps_count = filt.shape
        vmem = pl.BlockSpec(memory_space=pltpu.VMEM)
        hbm = pl.BlockSpec(memory_space=pltpu.HBM)
        dma = pltpu.SemaphoreType.DMA
        one = dma(())
        state = lambda count: pltpu.VMEM((count, 8, B), F32)
        plane = lambda kind: pltpu.VMEM((nt, B, B), kind)
        arguments = [
            pltpu.with_memory_space_constraint(value, pltpu.HBM)
            for value in (q_mr, k_mr, v_mr, q_li, k_li, cot, filt, gain.reshape(nt, B), decay.T, resid.T)
        ]
        shapes = [((rows, width), BF16)] * 6 + [((nt, B), F32), ((groups, taps_count), F32)]
        outs = pl.pallas_call(
            functools.partial(kernel, n_seq, n_chan, nt),
            out_shape=[jax.ShapeDtypeStruct(*shape) for shape in shapes],
            in_specs=[hbm] * 10,
            out_specs=[vmem] * 8,
            scratch_shapes=[pltpu.VMEM(value.shape, value.dtype) for value in arguments] + [
                pltpu.VMEM((nt, 2 * B, B), BF16), pltpu.VMEM((nt, 2 * B, B), BF16),
                pltpu.VMEM((nt, GT * B, 2 * B), BF16), pltpu.VMEM((nt, GT * B, 2 * B), BF16),
                pltpu.VMEM((nt, GT * B, B), BF16), pltpu.VMEM((nt, GT * B, B), BF16),
                plane(F32), plane(F32), plane(F32), plane(BF16), plane(BF16), plane(F32),
                pltpu.VMEM((nt, 2 * B, B), BF16), pltpu.VMEM((nt, 2 * B, B), BF16),
                pltpu.VMEM((nt, B, 2 * B), BF16), pltpu.VMEM((nt, B, 2 * B), BF16),
                pltpu.VMEM((2, nt * GT, B), F32), pltpu.VMEM((2, nt * GT, B), F32), state(units),
                state(units), state(n_seq), state(n_seq), state(units),
                state(units), state(n_seq), state(n_seq), state(units),
                state(n_chan), state(nt + 1), state(n_seq), state(1), state(nt + 1),
                dma((10,)), one, dma((nt,)), one, dma((nt,)),
                one, one, one, one, one, one, one, one, one, one, one, one, one, one,
            ],
            compiler_params=pltpu.CompilerParams(
                collective_id=0, has_side_effects=True, vmem_limit_bytes=40 * 1024 * 1024
            ),
        )(*arguments)
        outs = pl.pallas_call(
            deliver,
            out_shape=[jax.ShapeDtypeStruct(*shape) for shape in shapes],
            in_specs=[vmem] * 8,
            out_specs=[hbm] * 8,
            scratch_shapes=[dma((8,))],
            compiler_params=pltpu.CompilerParams(vmem_limit_bytes=1024 * 1024),
        )(*outs)
        return (*outs[:6], outs[6].reshape(width), outs[7])

    wide, by_group, by_chan = P("seq", "chan"), P("chan", None), P("chan")
    return jax.shard_map(
        on_device, mesh=mesh,
        in_specs=(wide,) * 6 + (by_group, by_chan, by_group, by_group),
        out_specs=(wide,) * 6 + (by_chan, by_group),
        check_vma=False,
    )
```

```python
import functools

import jax
import jax.numpy as jnp
from jax import lax
from jax.experimental import pallas as pl
from jax.experimental.pallas import tpu as pltpu
from jax.sharding import PartitionSpec as P

MESH = pl.DeviceIdType.MESH
F32 = jnp.float32
BF16 = jnp.bfloat16
B = 128
GS = 16
GT = B // GS
W = B + GS


def dot(a, b):
    return jnp.dot(a, b, preferred_element_type=F32)


def split(x):
    hi = x.astype(BF16)
    return hi, (x - hi.astype(F32)).astype(BF16)


def kernel(
    n_seq, n_chan, nt,
    q_mr_in, k_mr_in, v_mr_in, q_li_in, k_li_in, cot_in, filt_in, gain_in, decay_in, resid_in,
    out_li, g_qmr, g_kmr, g_vmr, g_qli, g_kli, g_gain, g_filt,
    q_mr, k_mr, v_mr, q_li, k_li, cot, filt, gain, decay, resid,
    ext, bext, tmf, tmb, tlf, tlb, conv, outm, gml, bli, xli, cli,
    winf, woutf, woutb, taps, rtaps, avec,
    bs_src, bs_dst, be_src, be_dst, fs_src, fs_dst, fe_src, fe_dst,
    pbuf, cbuf, r_src, r_dst, a_src, a_dst,
    in_sem, hf_s, hf_r, hb_s, hb_r, bs_s, bs_r, be_s, be_r, fs_s, fs_r, fe_s, fe_r,
    p_s, p_r, c_s, c_r, r_s, r_r, a_s, a_r,
):
    seq = lax.axis_index("seq")
    chan = lax.axis_index("chan")
    units = 2 * nt
    total = float(n_chan * nt * B)
    scale = float(n_seq * B) ** -0.5
    stride = n_seq // units
    owners_b = (0, stride, units)
    owners_f = (n_seq - 1 - stride * (units - 1), stride, units)
    owners_r = (0, n_seq // (nt + 1), nt + 1)

    lane = lax.broadcasted_iota(jnp.int32, (B, B), 1)
    row = lax.broadcasted_iota(jnp.int32, (B, B), 0)
    lane_group = lane >> 4
    diag_groups = (row >> 4) == lane_group
    eye = row == lane

    def cols(k):
        return pl.ds(pl.multiple_of(k * B, B), B)

    def tile(ref, k):
        return ref[:, cols(k)].astype(F32)

    lane_s = lax.broadcasted_iota(jnp.int32, (GS, B), 1)
    row_s = lax.broadcasted_iota(jnp.int32, (GS, B), 0)
    group_s = lane_s >> 4

    def windows(ref, k):
        return jnp.concatenate([ref[k, a * GS:a * GS + W, :] for a in range(GT)], axis=1)

    def banded(bands, ref, k):
        full = dot(bands[k], windows(ref, k))
        blocks = []
        for a in range(GT):
            part = full[:, a * B:(a + 1) * B]
            out = part[0:GS]
            for g in range(1, GT):
                out = jnp.where(group_s == g, part[g * GS:(g + 1) * GS], out)
            blocks.append(out)
        return jnp.concatenate(blocks, axis=0)

    def squeeze(full):
        return jnp.sum(jnp.where(diag_groups, full, 0.0).reshape(GT, GS, B), axis=0)

    def remote(src, dst, ss, rs, axis, target):
        return pltpu.make_async_remote_copy(
            src_ref=src, dst_ref=dst, send_sem=ss, recv_sem=rs,
            device_id={axis: target}, device_id_type=MESH,
        )

    fetches = [
        pltpu.make_async_copy(src, dst, in_sem.at[i])
        for i, (src, dst) in enumerate((
            (decay_in, decay), (cot_in, cot), (q_li_in, q_li), (k_mr_in, k_mr), (v_mr_in, v_mr),
            (resid_in, resid), (filt_in, filt), (gain_in, gain), (q_mr_in, q_mr), (k_li_in, k_li)))
    ]
    for fetch in fetches:
        fetch.start()

    barrier = pltpu.get_barrier_semaphore()

    @pl.loop(1, n_seq)
    def _(d):
        pl.semaphore_signal(barrier, inc=1, device_id={"seq": lax.rem(seq + d, n_seq)}, device_id_type=MESH)

    @pl.loop(1, n_chan)
    def _(d):
        pl.semaphore_signal(barrier, inc=1, device_id={"chan": lax.rem(chan + d, n_chan)}, device_id_type=MESH)

    time = lane.astype(F32)
    group_lane = lax.broadcasted_iota(jnp.int32, decay.shape, 1)

    def column(values, k):
        return jnp.concatenate([
            jnp.sum(jnp.where(group_lane == k * GT + g, values, 0.0), axis=1, keepdims=True) for g in range(GT)
        ], axis=0)

    for fetch in fetches[0:3]:
        fetch.wait()

    @pl.loop(0, nt, unroll=True)
    def _(k):
        hi, lo = split(jnp.exp(-column(decay[...], k) * time))
        back = (tile(cot, k) * tile(q_li, k)).astype(BF16)
        bli[k, 0:B, :] = back
        bli[k, B:2 * B, :] = jnp.zeros((B, B), BF16)
        xli[k, 0:B, :] = jnp.zeros((B, B), BF16)
        states = squeeze(dot(hi, back) + dot(lo, back))
        bs_src[2 * k] = states[0:8]
        bs_src[2 * k + 1] = states[8:16]

    pl.semaphore_wait(barrier, n_seq - 1 + n_chan - 1)

    def owns(owners):
        base, step, count = owners
        place = seq - base
        return jnp.logical_and(jnp.logical_and(place >= 0, place < step * count), lax.rem(place, step) == 0)

    def unit(owners):
        return lax.div(seq - owners[0], owners[1])

    def send_unit(src, dst, ss, rs, owners, u):
        owner = owners[0] + owners[1] * u

        @pl.when(seq != owner)
        def _():
            remote(src.at[u], dst.at[seq], ss, rs, "seq", owner).start()

        @pl.when(seq == owner)
        def _():
            dst[seq] = src[u]

    def scatter(src, dst, ss, rs, owners):
        @pl.loop(0, owners[2])
        def _(i):
            send_unit(src, dst, ss, rs, owners, lax.rem(seq + i, owners[2]))

    def answer(e_src, e_dst, es, er, u, one):
        @pl.loop(1, n_seq)
        def _(d):
            other = lax.rem(seq + d, n_seq)
            remote(e_src.at[0] if one else e_src.at[other], e_dst.at[u], es, er, "seq", other).start()

    def several(ref, ss, rs, count):
        return remote(ref.at[pl.ds(0, count)], ref.at[pl.ds(0, count)], ss, rs, "seq", lax.rem(seq + 1, n_seq))

    def but_own(owners, wait):
        count = owners[2]

        @pl.when(owns(owners))
        def _():
            wait(count - 1)

        @pl.when(jnp.logical_not(owns(owners)))
        def _():
            wait(count)

    def scatter_wait(src, ss, rs, owners):
        but_own(owners, lambda n: several(src, ss, rs, n).wait_send())

    def answer_wait(e_dst, es, er, owners):
        but_own(owners, lambda n: several(e_dst, es, er, n).wait_recv())

    def owner_wait(dst, ss, rs):
        several(dst, ss, rs, n_seq - 1).wait_recv()

    def owner_scan(dst, ss, rs, e_src, e_dst, es, er, owners, backward):
        @pl.when(owns(owners))
        def _():
            owner_wait(dst, ss, rs)
            u = unit(owners)
            fade = avec[u]

            def step(i, state):
                q = n_seq - 1 - i if backward else i
                e_src[q] = state
                return fade * state + dst[q]

            lax.fori_loop(0, n_seq, step, jnp.zeros((8, B), F32))
            e_dst[u] = e_src[seq]
            answer(e_src, e_dst, es, er, u, False)

    scatter(bs_src, bs_dst, bs_s, bs_r, owners_b)

    for fetch in fetches[3:5]:
        fetch.wait()

    @pl.loop(0, nt, unroll=True)
    def _(k):
        ext[k, B:2 * B, :] = (tile(k_mr, k) * tile(v_mr, k)).astype(BF16)

    def halo_f(k):
        return remote(ext.at[k, pl.ds(B, B)], ext.at[k, pl.ds(0, B)], hf_s, hf_r.at[k], "seq", lax.rem(seq + 1, n_seq))

    def halo_b(k):
        return remote(bext.at[k, pl.ds(0, B)], bext.at[k, pl.ds(B, B)], hb_s, hb_r.at[k], "seq",
                      lax.rem(seq + n_seq - 1, n_seq))

    @pl.when(seq < n_seq - 1)
    def _():
        @pl.loop(0, nt, unroll=True)
        def _(k):
            halo_f(k).start()

    @pl.when(seq == 0)
    def _():
        @pl.loop(0, nt, unroll=True)
        def _(k):
            ext[k, 0:B, :] = jnp.zeros((B, B), BF16)

    @pl.when(seq == n_seq - 1)
    def _():
        @pl.loop(0, nt, unroll=True)
        def _(k):
            bext[k, B:2 * B, :] = jnp.zeros((B, B), BF16)

    for fetch in fetches[5:]:
        fetch.wait()

    @pl.loop(0, nt, unroll=True)
    def _(k):
        rate = column(decay[...], k)
        weight = column(resid[...], k) * jnp.sqrt(2.0 * rate)
        fading = jnp.exp(-rate * time)
        powers = squeeze(jnp.broadcast_to(jnp.exp(-rate * float(B)), (B, B)))
        avec[2 * k] = powers[0:8]
        avec[2 * k + 1] = powers[8:16]
        taps[1, pl.ds(pl.multiple_of(k * GT, GT), GT), :] = jnp.sum((weight * fading).reshape(GT, GS, B), axis=1)
        hi, lo = split(jnp.exp(-rate * (B - 1.0 - time)))
        winf[k, 0:B, :] = hi
        winf[k, B:2 * B, :] = lo
        hi, lo = split((weight * jnp.exp(-rate * (B - time))).T)
        woutb[k, :, 0:B] = hi
        woutb[k, :, B:2 * B] = lo
        hi, lo = split((weight * jnp.exp(-rate * (time + 1.0))).T)
        woutf[k, :, 0:B] = hi
        woutf[k, :, B:2 * B] = lo

    reflect = jnp.where(row == ((B - lane) & (B - 1)), 1.0, 0.0)
    taps[0] = filt[...].astype(BF16).astype(F32)
    for which in range(2):
        rtaps[which] = dot(taps[which].astype(BF16), reflect.astype(BF16))

    @pl.loop(0, nt, unroll=True)
    def _(k):
        for ref, which, keep, out in (
            (taps, 1, lane_s >= row_s, tlb), (rtaps, 0, lane_s > row_s, tmf),
            (taps, 0, lane_s >= row_s, tmb), (rtaps, 1, lane_s > row_s, tlf),
        ):
            for g in range(GT):
                line = jnp.broadcast_to(ref[which, pl.ds(k * GT + g, 1), :], (GS, B))
                matrix = pltpu.roll(line, 0, axis=1, stride=1, stride_axis=0)
                out[k, g * GS:(g + 1) * GS, 0:B] = jnp.where(keep, matrix, 0.0).astype(BF16)
                out[k, g * GS:(g + 1) * GS, B:W] = jnp.where(keep, 0.0, matrix)[:, 0:GS].astype(BF16)

    def carried(wout, e_dst, k):
        state = jnp.concatenate([e_dst[2 * k], e_dst[2 * k + 1]], axis=0)
        hi, lo = split(jnp.where(diag_groups, jnp.concatenate([state] * GT, axis=0), 0.0))
        return dot(wout[k], jnp.concatenate([hi, hi], axis=0)) + dot(wout[k, :, 0:B], lo)

    @pl.loop(0, nt, unroll=True)
    def _(k):
        gml[k] = banded(tlb, bli, k)

    owner_scan(bs_dst, bs_s, bs_r, be_src, be_dst, be_s, be_r, owners_b, True)

    squares = jnp.zeros((B, B), F32)

    def mr_step(k, squares):
        @pl.when(seq > 0)
        def _():
            halo_f(k).wait_recv()

        value = banded(tmf, ext, k)
        conv[k] = value
        gated = (tile(q_mr, k) * value).astype(BF16).astype(F32)
        outm[k] = gated
        return squares + gated * gated

    squares = lax.fori_loop(0, nt, mr_step, squares, unroll=True)

    def as_row(partial):
        column = jnp.sum(partial, axis=1, keepdims=True)
        return jnp.sum(jnp.where(eye, column, 0.0), axis=0, keepdims=True)

    def as_column(line):
        return jnp.sum(jnp.where(eye, line, 0.0), axis=1, keepdims=True)

    def all_of(buf, ss, rs):
        part = buf.at[pl.ds(0, n_chan - 1)]
        return remote(part, part, ss, rs, "chan", lax.rem(chan + 1, n_chan))

    def psum_start(buf, partial, ss, rs):
        buf[chan] = jnp.broadcast_to(as_row(partial), (8, B))

        @pl.loop(1, n_chan)
        def _(d):
            remote(buf.at[chan], buf.at[chan], ss, rs, "chan", lax.rem(chan + d, n_chan)).start()

    def psum_end(buf, ss, rs):
        all_of(buf, ss, rs).wait_recv()
        sums = buf[0]
        for c in range(1, n_chan):
            sums = sums + buf[c]
        return sums[0:1]

    psum_start(pbuf, squares, p_s, p_r)
    inv_row = lax.rsqrt(psum_end(pbuf, p_s, p_r) / total + 1e-06)
    inv = as_column(inv_row)

    @pl.loop(0, nt, unroll=True)
    def _(k):
        normed = outm[k] * inv * gain[pl.ds(k, 1), :]
        mixed = (tile(k_li, k) * normed).astype(BF16)
        xli[k, B:2 * B, :] = mixed
        both = dot(winf[k], mixed)
        states = squeeze(both[0:B] + both[B:2 * B])
        fs_src[2 * k] = states[0:8]
        fs_src[2 * k + 1] = states[8:16]

    scatter(fs_src, fs_dst, fs_s, fs_r, owners_f)

    answer_wait(be_dst, be_s, be_r, owners_b)

    def li_step(k, cross):
        grad = gml[k] + carried(woutb, be_dst, k)
        gml[k] = grad
        return cross + grad * tile(k_li, k) * outm[k] * gain[pl.ds(k, 1), :]

    cross = lax.fori_loop(0, nt, li_step, jnp.zeros((B, B), F32), unroll=True)
    psum_start(cbuf, cross, c_s, c_r)

    @pl.loop(0, nt, unroll=True)
    def _(k):
        grad, scaled = gml[k], outm[k] * inv
        g_kli[:, cols(k)] = (grad * (scaled * gain[pl.ds(k, 1), :])).astype(BF16)
        r_src[nt, pl.ds(k, 1), :] = jnp.sum(grad * tile(k_li, k) * scaled, axis=0, keepdims=True)
        cli[k] = banded(tlf, xli, k)

    if nt < 8:
        r_src[nt, nt:8, :] = jnp.zeros((8 - nt, B), F32)
    send_unit(r_src, r_dst, r_s, r_r, owners_r, nt)

    pull = as_column(inv_row * inv_row * inv_row * psum_end(cbuf, c_s, c_r) / total)

    @pl.loop(0, nt, unroll=True)
    def _(k):
        grad_out = inv * (gml[k] * tile(k_li, k) * gain[pl.ds(k, 1), :]) - outm[k] * pull
        bext[k, 0:B, :] = (grad_out * tile(q_mr, k)).astype(BF16)

        @pl.when(seq > 0)
        def _():
            halo_b(k).start()

        g_qmr[:, cols(k)] = (grad_out * conv[k]).astype(BF16)

    row64 = lax.broadcasted_iota(jnp.int32, (8 * GT, B), 0)

    @pl.loop(0, nt, unroll=True)
    def _(k):
        back = bext[k, 0:B, :]
        masked = jnp.concatenate([
            jnp.concatenate([
                jnp.where(group_s == g, back[a * GS:(a + 1) * GS], jnp.zeros((GS, B), BF16)) for a in range(GT)
            ], axis=1) for g in range(GT)
        ], axis=0)
        gram = lax.dot_general(masked, windows(ext, k), (((1,), (1,)), ((), ())), preferred_element_type=F32)
        wrapped = jnp.concatenate([gram[:, B:W], jnp.zeros((B, B - GS), F32)], axis=1)
        cyclic = jnp.where(lane <= (row & (GS - 1)), wrapped, gram[:, 0:B])
        sums = [
            cyclic[g * GS:g * GS + 8] + pltpu.roll(cyclic[g * GS + 8:(g + 1) * GS], B - 8, axis=1) for g in range(GT)
        ]
        acc = jnp.concatenate(sums, axis=0)
        for bit in range(3):
            acc = jnp.where(((row64 >> bit) & 1) == 1, pltpu.roll(acc, B - (1 << bit), axis=1), acc)
        diagonals = jnp.sum(acc.reshape(GT, 8, B), axis=1)
        hi = diagonals.astype(BF16)
        rest = diagonals - hi.astype(F32)
        mid, lo = split(rest)
        parts = dot(jnp.concatenate([hi.astype(F32), mid.astype(F32), lo.astype(F32)], axis=0).astype(BF16),
                    reflect.astype(BF16))
        r_src[k] = parts[0:8] + parts[8:16] + parts[16:24]
        send_unit(r_src, r_dst, r_s, r_r, owners_r, k)

    owner_scan(fs_dst, fs_s, fs_r, fe_src, fe_dst, fe_s, fe_r, owners_f, False)

    @pl.when(owns(owners_r))
    def _():
        owner_wait(r_dst, r_s, r_r)
        u = unit(owners_r)
        result = lax.fori_loop(1, n_seq, lambda q, acc: acc + r_dst[q], r_dst[0]) * scale
        a_src[0] = result
        a_dst[u] = result
        answer(a_src, a_dst, a_s, a_r, u, True)

    answer_wait(fe_dst, fe_s, fe_r, owners_f)

    @pl.loop(0, nt, unroll=True)
    def _(k):
        value = cli[k] + carried(woutf, fe_dst, k)
        out_li[:, cols(k)] = (tile(q_li, k) * value).astype(BF16)
        g_qli[:, cols(k)] = (tile(cot, k) * value).astype(BF16)

    @pl.loop(0, nt, unroll=True)
    def _(k):
        @pl.when(seq < n_seq - 1)
        def _():
            halo_b(k).wait_recv()

        grad = banded(tmb, bext, k)
        g_kmr[:, cols(k)] = (grad * tile(v_mr, k)).astype(BF16)
        g_vmr[:, cols(k)] = (grad * tile(k_mr, k)).astype(BF16)

    answer_wait(a_dst, a_s, a_r, owners_r)
    for k in range(nt):
        g_filt[k * 8:(k + 1) * 8, :] = a_dst[k]
    g_gain[...] = a_dst[nt, 0:nt, :]

    @pl.when(seq < n_seq - 1)
    def _():
        remote(ext.at[:, pl.ds(B, B)], ext.at[:, pl.ds(0, B)], hf_s, hf_r.at[0], "seq", lax.rem(seq + 1, n_seq)).wait_send()

    @pl.when(seq > 0)
    def _():
        remote(bext.at[:, pl.ds(0, B)], bext.at[:, pl.ds(B, B)], hb_s, hb_r.at[0], "seq",
               lax.rem(seq + n_seq - 1, n_seq)).wait_send()

    scatter_wait(bs_src, bs_s, bs_r, owners_b)
    scatter_wait(fs_src, fs_s, fs_r, owners_f)
    scatter_wait(r_src, r_s, r_r, owners_r)
    for e_src, es, er, owners in ((be_src, be_s, be_r, owners_b), (fe_src, fe_s, fe_r, owners_f)):
        @pl.when(owns(owners))
        def _():
            several(e_src, es, er, n_seq - 1).wait_send()

    @pl.when(owns(owners_r))
    def _():
        several(r_dst, a_s, a_r, n_seq - 1).wait_send()

    all_of(pbuf, p_s, p_r).wait_send()
    all_of(cbuf, c_s, c_r).wait_send()


def deliver(*refs):
    count = len(refs) // 2
    sem = refs[-1]
    copies = [pltpu.make_async_copy(refs[i], refs[count + i], sem.at[i]) for i in range(count)]
    for copy in copies:
        copy.start()
    for copy in copies:
        copy.wait()


def solution(mesh):
    n_seq, n_chan = mesh.shape["seq"], mesh.shape["chan"]

    def on_device(q_mr, k_mr, v_mr, q_li, k_li, cot, filt, gain, decay, resid):
        rows, width = q_mr.shape
        nt = width // B
        units = 2 * nt
        groups, taps_count = filt.shape
        vmem = pl.BlockSpec(memory_space=pltpu.VMEM)
        hbm = pl.BlockSpec(memory_space=pltpu.HBM)
        dma = pltpu.SemaphoreType.DMA
        one = dma(())
        state = lambda count: pltpu.VMEM((count, 8, B), F32)
        plane = lambda kind: pltpu.VMEM((nt, B, B), kind)
        arguments = [
            pltpu.with_memory_space_constraint(value, pltpu.HBM)
            for value in (q_mr, k_mr, v_mr, q_li, k_li, cot, filt, gain.reshape(nt, B), decay.T, resid.T)
        ]
        shapes = [((rows, width), BF16)] * 6 + [((nt, B), F32), ((groups, taps_count), F32)]
        outs = pl.pallas_call(
            functools.partial(kernel, n_seq, n_chan, nt),
            out_shape=[jax.ShapeDtypeStruct(*shape) for shape in shapes],
            in_specs=[hbm] * 10,
            out_specs=[vmem] * 8,
            scratch_shapes=[pltpu.VMEM(value.shape, value.dtype) for value in arguments] + [
                pltpu.VMEM((nt, 2 * B, B), BF16), pltpu.VMEM((nt, 2 * B, B), BF16),
                pltpu.VMEM((nt, B, W), BF16), pltpu.VMEM((nt, B, W), BF16),
                pltpu.VMEM((nt, B, W), BF16), pltpu.VMEM((nt, B, W), BF16),
                plane(F32), plane(F32), plane(F32), pltpu.VMEM((nt, 2 * B, B), BF16), pltpu.VMEM((nt, 2 * B, B), BF16), plane(F32),
                pltpu.VMEM((nt, 2 * B, B), BF16),
                pltpu.VMEM((nt, B, 2 * B), BF16), pltpu.VMEM((nt, B, 2 * B), BF16),
                pltpu.VMEM((2, nt * GT, B), F32), pltpu.VMEM((2, nt * GT, B), F32), state(units),
                state(units), state(n_seq), state(n_seq), state(units),
                state(units), state(n_seq), state(n_seq), state(units),
                state(n_chan), state(n_chan), state(nt + 1), state(n_seq), state(1), state(nt + 1),
                dma((10,)), one, dma((nt,)), one, dma((nt,)),
                one, one, one, one, one, one, one, one, one, one, one, one, one, one, one, one,
            ],
            compiler_params=pltpu.CompilerParams(
                collective_id=0, has_side_effects=True, vmem_limit_bytes=40 * 1024 * 1024
            ),
        )(*arguments)
        outs = pl.pallas_call(
            deliver,
            out_shape=[jax.ShapeDtypeStruct(*shape) for shape in shapes],
            in_specs=[vmem] * 8,
            out_specs=[hbm] * 8,
            scratch_shapes=[dma((8,))],
            compiler_params=pltpu.CompilerParams(vmem_limit_bytes=1024 * 1024),
        )(*outs)
        return (*outs[:6], outs[6].reshape(width), outs[7])

    wide, by_group, by_chan = P("seq", "chan"), P("chan", None), P("chan")
    return jax.shard_map(
        on_device, mesh=mesh,
        in_specs=(wide,) * 6 + (by_group, by_chan, by_group, by_group),
        out_specs=(wide,) * 6 + (by_chan, by_group),
        check_vma=False,
    )
```

```python
import functools

import jax
import jax.numpy as jnp
from jax import lax
from jax.experimental import pallas as pl
from jax.experimental.pallas import tpu as pltpu
from jax.sharding import PartitionSpec as P

MESH = pl.DeviceIdType.MESH
F32 = jnp.float32
BF16 = jnp.bfloat16
B = 128
GS = 16
GT = B // GS
W = B + GS


def dot(a, b):
    return jnp.dot(a, b, preferred_element_type=F32)


def split(x):
    hi = x.astype(BF16)
    return hi, (x - hi.astype(F32)).astype(BF16)


def kernel(
    n_seq, n_chan, nt,
    q_mr_in, k_mr_in, v_mr_in, q_li_in, k_li_in, cot_in, filt_in, gain_in, decay_in, resid_in,
    out_li, g_qmr, g_kmr, g_vmr, g_qli, g_kli, g_gain, g_filt,
    q_mr, k_mr, v_mr, q_li, k_li, cot, filt, gain, decay, resid,
    ext, bext, tmf, tmb, tlf, tlb, conv, outm, gml, bli, xli, cli,
    winf, woutf, woutb, taps, rtaps, avec,
    bs_src, bs_dst, be_src, be_dst, fs_src, fs_dst, fe_src, fe_dst,
    pbuf, cbuf, r_src, r_dst, a_src, a_dst,
    in_sem, hf_s, hf_r, hb_s, hb_r, bs_s, bs_r, be_s, be_r, fs_s, fs_r, fe_s, fe_r,
    p_s, p_r, c_s, c_r, r_s, r_r, a_s, a_r,
):
    seq = lax.axis_index("seq")
    chan = lax.axis_index("chan")
    units = 2 * nt
    total = float(n_chan * nt * B)
    scale = float(n_seq * B) ** -0.5
    stride = n_seq // units
    owners_b = (0, stride, units)
    owners_f = (n_seq - 1 - stride * (units - 1), stride, units)
    sums_r = nt // 2 + 1
    owners_r = (0, n_seq // sums_r, sums_r)
    nz = 8 if n_seq % 8 == 0 else n_seq
    ny = n_seq // nz
    my_y, my_z = lax.div(seq, nz), lax.rem(seq, nz)

    def ring_order(i, n):
        return lax.rem(n // 2 + n + lax.div(i + 1, 2) * (1 - 2 * lax.rem(i, 2)), n)

    def far_first(i):
        dy, dz = ring_order(lax.rem(i, ny), ny), ring_order(lax.div(i, ny), nz)
        return lax.rem(my_y + dy, ny) * nz + lax.rem(my_z + dz, nz)

    def far_first_unit(i, count):
        wide = count // ny
        dy, dz = ring_order(lax.rem(i, ny), ny), ring_order(lax.div(i, ny), wide)
        return lax.rem(my_y + dy, ny) * wide + lax.rem(lax.div(my_z * wide, nz) + dz, wide)

    lane = lax.broadcasted_iota(jnp.int32, (B, B), 1)
    row = lax.broadcasted_iota(jnp.int32, (B, B), 0)
    lane_group = lane >> 4
    diag_groups = (row >> 4) == lane_group
    eye = row == lane

    def cols(k):
        return pl.ds(pl.multiple_of(k * B, B), B)

    def tile(ref, k):
        return ref[:, cols(k)].astype(F32)

    lane_s = lax.broadcasted_iota(jnp.int32, (GS, B), 1)
    row_s = lax.broadcasted_iota(jnp.int32, (GS, B), 0)
    group_s = lane_s >> 4

    def windows(ref, k):
        return jnp.concatenate([ref[k, a * GS:a * GS + W, :] for a in range(GT)], axis=1)

    def banded(bands, ref, k):
        full = dot(bands[k], windows(ref, k))
        blocks = []
        for a in range(GT):
            part = full[:, a * B:(a + 1) * B]
            out = part[0:GS]
            for g in range(1, GT):
                out = jnp.where(group_s == g, part[g * GS:(g + 1) * GS], out)
            blocks.append(out)
        return jnp.concatenate(blocks, axis=0)

    def squeeze(full):
        return jnp.sum(jnp.where(diag_groups, full, 0.0).reshape(GT, GS, B), axis=0)

    def remote(src, dst, ss, rs, axis, target):
        return pltpu.make_async_remote_copy(
            src_ref=src, dst_ref=dst, send_sem=ss, recv_sem=rs,
            device_id={axis: target}, device_id_type=MESH,
        )

    barrier = pltpu.get_barrier_semaphore()

    @pl.loop(0, n_seq - 1)
    def _(i):
        pl.semaphore_signal(barrier, inc=1, device_id={"seq": far_first(i)}, device_id_type=MESH)

    @pl.loop(1, n_chan)
    def _(d):
        pl.semaphore_signal(barrier, inc=1, device_id={"chan": lax.rem(chan + d, n_chan)}, device_id_type=MESH)

    fetches = [
        pltpu.make_async_copy(src, dst, in_sem.at[i])
        for i, (src, dst) in enumerate((
            (decay_in, decay), (cot_in, cot), (q_li_in, q_li), (k_mr_in, k_mr), (v_mr_in, v_mr),
            (resid_in, resid), (filt_in, filt), (gain_in, gain), (q_mr_in, q_mr), (k_li_in, k_li)))
    ]
    for fetch in fetches:
        fetch.start()

    time = lane.astype(F32)
    group_lane = lax.broadcasted_iota(jnp.int32, decay.shape, 1)

    def column(values, k):
        return jnp.concatenate([
            jnp.sum(jnp.where(group_lane == k * GT + g, values, 0.0), axis=1, keepdims=True) for g in range(GT)
        ], axis=0)

    for fetch in fetches[0:3]:
        fetch.wait()

    @pl.loop(0, nt, unroll=True)
    def _(k):
        hi, lo = split(jnp.exp(-column(decay[...], k) * time))
        back = (tile(cot, k) * tile(q_li, k)).astype(BF16)
        bli[k, 0:B, :] = back
        bli[k, B:2 * B, :] = jnp.zeros((B, B), BF16)
        xli[k, 0:B, :] = jnp.zeros((B, B), BF16)
        states = squeeze(dot(hi, back) + dot(lo, back))
        bs_src[2 * k] = states[0:8]
        bs_src[2 * k + 1] = states[8:16]

    pl.semaphore_wait(barrier, n_seq - 1 + n_chan - 1)

    def owns(owners):
        base, step, count = owners
        place = seq - base
        return jnp.logical_and(jnp.logical_and(place >= 0, place < step * count), lax.rem(place, step) == 0)

    def unit(owners):
        return lax.div(seq - owners[0], owners[1])

    def send_unit(src, dst, ss, rs, owners, u):
        owner = owners[0] + owners[1] * u

        @pl.when(seq != owner)
        def _():
            remote(src.at[u], dst.at[seq], ss, rs, "seq", owner).start()

        @pl.when(seq == owner)
        def _():
            dst[seq] = src[u]

    def scatter(src, dst, ss, rs, owners):
        @pl.loop(0, owners[2])
        def _(i):
            send_unit(src, dst, ss, rs, owners, far_first_unit(i, owners[2]))

    def answer(e_src, e_dst, es, er, u, one):
        @pl.loop(0, n_seq - 1)
        def _(i):
            other = far_first(i)
            remote(e_src.at[0] if one else e_src.at[other], e_dst.at[u], es, er, "seq", other).start()

    def several(ref, ss, rs, count):
        return remote(ref.at[pl.ds(0, count)], ref.at[pl.ds(0, count)], ss, rs, "seq", lax.rem(seq + 1, n_seq))

    def but_own(owners, wait):
        count = owners[2]

        @pl.when(owns(owners))
        def _():
            wait(count - 1)

        @pl.when(jnp.logical_not(owns(owners)))
        def _():
            wait(count)

    def scatter_wait(src, ss, rs, owners):
        but_own(owners, lambda n: several(src, ss, rs, n).wait_send())

    def answer_wait(e_dst, es, er, owners):
        but_own(owners, lambda n: several(e_dst, es, er, n).wait_recv())

    def owner_wait(dst, ss, rs):
        several(dst, ss, rs, n_seq - 1).wait_recv()

    def owner_scan(dst, ss, rs, e_src, e_dst, es, er, owners, backward):
        @pl.when(owns(owners))
        def _():
            owner_wait(dst, ss, rs)
            u = unit(owners)
            fade = avec[u]

            def step(i, state):
                q = n_seq - 1 - i if backward else i
                e_src[q] = state
                return fade * state + dst[q]

            lax.fori_loop(0, n_seq, step, jnp.zeros((8, B), F32), unroll=8 if n_seq % 8 == 0 else 1)
            e_dst[u] = e_src[seq]
            answer(e_src, e_dst, es, er, u, False)

    scatter(bs_src, bs_dst, bs_s, bs_r, owners_b)

    for fetch in fetches[3:5]:
        fetch.wait()

    @pl.loop(0, nt, unroll=True)
    def _(k):
        ext[k, B:2 * B, :] = (tile(k_mr, k) * tile(v_mr, k)).astype(BF16)

    def halo_f(k):
        return remote(ext.at[k, pl.ds(B, B)], ext.at[k, pl.ds(0, B)], hf_s, hf_r.at[k], "seq", lax.rem(seq + 1, n_seq))

    def halo_b(k):
        return remote(bext.at[k, pl.ds(0, B)], bext.at[k, pl.ds(B, B)], hb_s, hb_r.at[k], "seq",
                      lax.rem(seq + n_seq - 1, n_seq))

    @pl.when(seq < n_seq - 1)
    def _():
        @pl.loop(0, nt, unroll=True)
        def _(k):
            halo_f(k).start()

    @pl.when(seq == 0)
    def _():
        @pl.loop(0, nt, unroll=True)
        def _(k):
            ext[k, 0:B, :] = jnp.zeros((B, B), BF16)

    @pl.when(seq == n_seq - 1)
    def _():
        @pl.loop(0, nt, unroll=True)
        def _(k):
            bext[k, B:2 * B, :] = jnp.zeros((B, B), BF16)

    for fetch in fetches[5:]:
        fetch.wait()

    @pl.loop(0, nt, unroll=True)
    def _(k):
        rate = column(decay[...], k)
        weight = column(resid[...], k) * jnp.sqrt(2.0 * rate)
        fading = jnp.exp(-rate * time)
        powers = squeeze(jnp.broadcast_to(jnp.exp(-rate * float(B)), (B, B)))
        avec[2 * k] = powers[0:8]
        avec[2 * k + 1] = powers[8:16]
        taps[1, pl.ds(pl.multiple_of(k * GT, GT), GT), :] = jnp.sum((weight * fading).reshape(GT, GS, B), axis=1)
        hi, lo = split(jnp.exp(-rate * (B - 1.0 - time)))
        winf[k, 0:B, :] = hi
        winf[k, B:2 * B, :] = lo
        hi, lo = split((weight * jnp.exp(-rate * (B - time))).T)
        woutb[k, :, 0:B] = hi
        woutb[k, :, B:2 * B] = lo
        hi, lo = split((weight * jnp.exp(-rate * (time + 1.0))).T)
        woutf[k, :, 0:B] = hi
        woutf[k, :, B:2 * B] = lo

    reflect = jnp.where(row == ((B - lane) & (B - 1)), 1.0, 0.0)
    taps[0] = filt[...].astype(BF16).astype(F32)
    for which in range(2):
        rtaps[which] = dot(taps[which].astype(BF16), reflect.astype(BF16))

    @pl.loop(0, nt, unroll=True)
    def _(k):
        for ref, which, keep, out in (
            (taps, 1, lane_s >= row_s, tlb), (rtaps, 0, lane_s > row_s, tmf),
            (taps, 0, lane_s >= row_s, tmb), (rtaps, 1, lane_s > row_s, tlf),
        ):
            for g in range(GT):
                line = jnp.broadcast_to(ref[which, pl.ds(k * GT + g, 1), :], (GS, B))
                matrix = pltpu.roll(line, 0, axis=1, stride=1, stride_axis=0)
                out[k, g * GS:(g + 1) * GS, 0:B] = jnp.where(keep, matrix, 0.0).astype(BF16)
                out[k, g * GS:(g + 1) * GS, B:W] = jnp.where(keep, 0.0, matrix)[:, 0:GS].astype(BF16)

    def carried(wout, e_dst, k):
        state = jnp.concatenate([e_dst[2 * k], e_dst[2 * k + 1]], axis=0)
        hi, lo = split(jnp.where(diag_groups, jnp.concatenate([state] * GT, axis=0), 0.0))
        return dot(wout[k], jnp.concatenate([hi, hi], axis=0)) + dot(wout[k, :, 0:B], lo)

    @pl.loop(0, nt, unroll=True)
    def _(k):
        gml[k] = banded(tlb, bli, k)

    owner_scan(bs_dst, bs_s, bs_r, be_src, be_dst, be_s, be_r, owners_b, True)

    squares = jnp.zeros((B, B), F32)

    def mr_step(k, squares):
        @pl.when(seq > 0)
        def _():
            halo_f(k).wait_recv()

        value = banded(tmf, ext, k)
        conv[k] = value
        gated = (tile(q_mr, k) * value).astype(BF16).astype(F32)
        outm[k] = gated
        return squares + gated * gated

    squares = lax.fori_loop(0, nt, mr_step, squares, unroll=True)

    def as_row(partial):
        column = jnp.sum(partial, axis=1, keepdims=True)
        return jnp.sum(jnp.where(eye, column, 0.0), axis=0, keepdims=True)

    def as_column(line):
        return jnp.sum(jnp.where(eye, line, 0.0), axis=1, keepdims=True)

    def all_of(buf, ss, rs):
        part = buf.at[pl.ds(0, n_chan - 1), pl.ds(0, 1)]
        return remote(part, part, ss, rs, "chan", lax.rem(chan + 1, n_chan))

    def psum_start(buf, partial, ss, rs):
        buf[chan, 0:1, :] = as_row(partial)
        mine = buf.at[chan, pl.ds(0, 1)]

        @pl.loop(1, n_chan)
        def _(d):
            remote(mine, mine, ss, rs, "chan", lax.rem(chan + d, n_chan)).start()

    def psum_end(buf, ss, rs):
        all_of(buf, ss, rs).wait_recv()
        sums = buf[0, 0:1, :]
        for c in range(1, n_chan):
            sums = sums + buf[c, 0:1, :]
        return sums

    psum_start(pbuf, squares, p_s, p_r)
    inv_row = lax.rsqrt(psum_end(pbuf, p_s, p_r) / total + 1e-06)
    inv = as_column(inv_row)

    @pl.loop(0, nt, unroll=True)
    def _(k):
        normed = outm[k] * inv * gain[pl.ds(k, 1), :]
        mixed = (tile(k_li, k) * normed).astype(BF16)
        xli[k, B:2 * B, :] = mixed
        both = dot(winf[k], mixed)
        states = squeeze(both[0:B] + both[B:2 * B])
        fs_src[2 * k] = states[0:8]
        fs_src[2 * k + 1] = states[8:16]

    scatter(fs_src, fs_dst, fs_s, fs_r, owners_f)

    answer_wait(be_dst, be_s, be_r, owners_b)

    def li_step(k, cross):
        grad = gml[k] + carried(woutb, be_dst, k)
        gml[k] = grad
        return cross + grad * tile(k_li, k) * outm[k] * gain[pl.ds(k, 1), :]

    cross = lax.fori_loop(0, nt, li_step, jnp.zeros((B, B), F32), unroll=True)
    psum_start(cbuf, cross, c_s, c_r)

    gains = []
    for k in range(nt):
        grad, scaled = gml[k], outm[k] * inv
        g_kli[:, cols(k)] = (grad * (scaled * gain[pl.ds(k, 1), :])).astype(BF16)
        gains.append(jnp.sum(grad * tile(k_li, k) * scaled, axis=0, keepdims=True))
        cli[k] = banded(tlf, xli, k)
    gains.append(jnp.zeros((16 - nt, B), F32))
    r_src[nt // 2] = jnp.concatenate(gains, axis=0).astype(BF16)
    send_unit(r_src, r_dst, r_s, r_r, owners_r, nt // 2)

    pull = as_column(inv_row * inv_row * inv_row * psum_end(cbuf, c_s, c_r) / total)

    @pl.loop(0, nt, unroll=True)
    def _(k):
        grad_out = inv * (gml[k] * tile(k_li, k) * gain[pl.ds(k, 1), :]) - outm[k] * pull
        bext[k, 0:B, :] = (grad_out * tile(q_mr, k)).astype(BF16)

        g_qmr[:, cols(k)] = (grad_out * conv[k]).astype(BF16)

    row64 = lax.broadcasted_iota(jnp.int32, (8 * GT, B), 0)

    halves = []
    for k in range(nt):
        back = bext[k, 0:B, :]
        masked = jnp.concatenate([
            jnp.concatenate([
                jnp.where(group_s == g, back[a * GS:(a + 1) * GS], jnp.zeros((GS, B), BF16)) for a in range(GT)
            ], axis=1) for g in range(GT)
        ], axis=0)
        gram = lax.dot_general(masked, windows(ext, k), (((1,), (1,)), ((), ())), preferred_element_type=F32)
        wrapped = jnp.concatenate([gram[:, B:W], jnp.zeros((B, B - GS), F32)], axis=1)
        cyclic = jnp.where(lane <= (row & (GS - 1)), wrapped, gram[:, 0:B])
        sums = [
            cyclic[g * GS:g * GS + 8] + pltpu.roll(cyclic[g * GS + 8:(g + 1) * GS], B - 8, axis=1) for g in range(GT)
        ]
        acc = jnp.concatenate(sums, axis=0)
        for bit in range(3):
            acc = jnp.where(((row64 >> bit) & 1) == 1, pltpu.roll(acc, B - (1 << bit), axis=1), acc)
        halves.append(jnp.sum(acc.reshape(GT, 8, B), axis=1))
        if k % 2:
            r_src[k // 2] = jnp.concatenate(halves[-2:], axis=0).astype(BF16)
            send_unit(r_src, r_dst, r_s, r_r, owners_r, k // 2)

    owner_scan(fs_dst, fs_s, fs_r, fe_src, fe_dst, fe_s, fe_r, owners_f, False)

    @pl.when(seq > 0)
    def _():
        @pl.loop(0, nt)
        def _(k):
            halo_b(k).start()

    @pl.when(owns(owners_r))
    def _():
        owner_wait(r_dst, r_s, r_r)
        u = unit(owners_r)
        result = jnp.sum(r_dst[...].astype(F32), axis=0).astype(BF16)
        a_src[0] = result
        a_dst[u] = result
        answer(a_src, a_dst, a_s, a_r, u, True)

    answer_wait(fe_dst, fe_s, fe_r, owners_f)

    @pl.loop(0, nt, unroll=True)
    def _(k):
        value = cli[k] + carried(woutf, fe_dst, k)
        out_li[:, cols(k)] = (tile(q_li, k) * value).astype(BF16)
        g_qli[:, cols(k)] = (tile(cot, k) * value).astype(BF16)

    @pl.loop(0, nt, unroll=True)
    def _(k):
        @pl.when(seq < n_seq - 1)
        def _():
            halo_b(k).wait_recv()

        grad = banded(tmb, bext, k)
        g_kmr[:, cols(k)] = (grad * tile(v_mr, k)).astype(BF16)
        g_vmr[:, cols(k)] = (grad * tile(k_mr, k)).astype(BF16)

    answer_wait(a_dst, a_s, a_r, owners_r)
    sums = jnp.concatenate([a_dst[u] for u in range(nt // 2)], axis=0)
    g_filt[...] = dot(sums, reflect.astype(BF16)) * scale
    g_gain[...] = a_dst[nt // 2].astype(F32)[0:nt] * scale

    @pl.when(seq < n_seq - 1)
    def _():
        remote(ext.at[:, pl.ds(B, B)], ext.at[:, pl.ds(0, B)], hf_s, hf_r.at[0], "seq", lax.rem(seq + 1, n_seq)).wait_send()

    @pl.when(seq > 0)
    def _():
        remote(bext.at[:, pl.ds(0, B)], bext.at[:, pl.ds(B, B)], hb_s, hb_r.at[0], "seq",
               lax.rem(seq + n_seq - 1, n_seq)).wait_send()

    scatter_wait(bs_src, bs_s, bs_r, owners_b)
    scatter_wait(fs_src, fs_s, fs_r, owners_f)
    scatter_wait(r_src, r_s, r_r, owners_r)
    for e_src, es, er, owners in ((be_src, be_s, be_r, owners_b), (fe_src, fe_s, fe_r, owners_f)):
        @pl.when(owns(owners))
        def _():
            several(e_src, es, er, n_seq - 1).wait_send()

    @pl.when(owns(owners_r))
    def _():
        several(r_dst, a_s, a_r, n_seq - 1).wait_send()

    all_of(pbuf, p_s, p_r).wait_send()
    all_of(cbuf, c_s, c_r).wait_send()


def deliver(*refs):
    count = len(refs) // 2
    sem = refs[-1]
    copies = [pltpu.make_async_copy(refs[i], refs[count + i], sem.at[i]) for i in range(count)]
    for copy in copies:
        copy.start()
    for copy in copies:
        copy.wait()


def solution(mesh):
    n_seq, n_chan = mesh.shape["seq"], mesh.shape["chan"]

    def on_device(q_mr, k_mr, v_mr, q_li, k_li, cot, filt, gain, decay, resid):
        rows, width = q_mr.shape
        nt = width // B
        units = 2 * nt
        groups, taps_count = filt.shape
        vmem = pl.BlockSpec(memory_space=pltpu.VMEM)
        hbm = pl.BlockSpec(memory_space=pltpu.HBM)
        dma = pltpu.SemaphoreType.DMA
        one = dma(())
        state = lambda count: pltpu.VMEM((count, 8, B), F32)
        part = lambda count: pltpu.VMEM((count, 16, B), BF16)
        plane = lambda kind: pltpu.VMEM((nt, B, B), kind)
        arguments = [
            pltpu.with_memory_space_constraint(value, pltpu.HBM)
            for value in (q_mr, k_mr, v_mr, q_li, k_li, cot, filt, gain.reshape(nt, B), decay.T, resid.T)
        ]
        shapes = [((rows, width), BF16)] * 6 + [((nt, B), F32), ((groups, taps_count), F32)]
        outs = pl.pallas_call(
            functools.partial(kernel, n_seq, n_chan, nt),
            out_shape=[jax.ShapeDtypeStruct(*shape) for shape in shapes],
            in_specs=[hbm] * 10,
            out_specs=[vmem] * 8,
            scratch_shapes=[pltpu.VMEM(value.shape, value.dtype) for value in arguments] + [
                pltpu.VMEM((nt, 2 * B, B), BF16), pltpu.VMEM((nt, 2 * B, B), BF16),
                pltpu.VMEM((nt, B, W), BF16), pltpu.VMEM((nt, B, W), BF16),
                pltpu.VMEM((nt, B, W), BF16), pltpu.VMEM((nt, B, W), BF16),
                plane(F32), plane(F32), plane(F32), pltpu.VMEM((nt, 2 * B, B), BF16), pltpu.VMEM((nt, 2 * B, B), BF16), plane(F32),
                pltpu.VMEM((nt, 2 * B, B), BF16),
                pltpu.VMEM((nt, B, 2 * B), BF16), pltpu.VMEM((nt, B, 2 * B), BF16),
                pltpu.VMEM((2, nt * GT, B), F32), pltpu.VMEM((2, nt * GT, B), F32), state(units),
                state(units), state(n_seq), state(n_seq), state(units),
                state(units), state(n_seq), state(n_seq), state(units),
                state(n_chan), state(n_chan), part(nt // 2 + 1), part(n_seq), part(1), part(nt // 2 + 1),
                dma((10,)), one, dma((nt,)), one, dma((nt,)),
                one, one, one, one, one, one, one, one, one, one, one, one, one, one, one, one,
            ],
            compiler_params=pltpu.CompilerParams(
                collective_id=0, has_side_effects=True, vmem_limit_bytes=40 * 1024 * 1024
            ),
        )(*arguments)
        outs = pl.pallas_call(
            deliver,
            out_shape=[jax.ShapeDtypeStruct(*shape) for shape in shapes],
            in_specs=[vmem] * 8,
            out_specs=[hbm] * 8,
            scratch_shapes=[dma((8,))],
            compiler_params=pltpu.CompilerParams(vmem_limit_bytes=1024 * 1024),
        )(*outs)
        return (*outs[:6], outs[6].reshape(width), outs[7])

    wide, by_group, by_chan = P("seq", "chan"), P("chan", None), P("chan")
    return jax.shard_map(
        on_device, mesh=mesh,
        in_specs=(wide,) * 6 + (by_group, by_chan, by_group, by_group),
        out_specs=(wide,) * 6 + (by_chan, by_group),
        check_vma=False,
    )
```

```python
import functools

import jax
import jax.numpy as jnp
from jax import lax
from jax.experimental import pallas as pl
from jax.experimental.pallas import tpu as pltpu
from jax.sharding import PartitionSpec as P

MESH = pl.DeviceIdType.MESH
F32 = jnp.float32
BF16 = jnp.bfloat16
B = 128
GS = 16
GT = B // GS
W = B + GS


def dot(a, b):
    return jnp.dot(a, b, preferred_element_type=F32)


def split(x):
    hi = x.astype(BF16)
    return hi, (x - hi.astype(F32)).astype(BF16)


def kernel(
    n_seq, n_chan, nt,
    q_mr_in, k_mr_in, v_mr_in, q_li_in, k_li_in, cot_in, filt_in, gain_in, decay_in, resid_in,
    out_li, g_qmr, g_kmr, g_vmr, g_qli, g_kli, g_gain, g_filt,
    q_mr, k_mr, v_mr, q_li, k_li, cot, filt, gain, decay, resid,
    ext, bext, tmf, tmb, tlf, tlb, conv, outm, gml, bli, xli, cli,
    winf, woutf, woutb, taps, rtaps, avec,
    bs_src, bs_dst, be_src, be_dst, fs_src, fs_dst, fe_src, fe_dst,
    pbuf, cbuf, r_src, r_dst, a_src, a_dst,
    in_sem, hf_s, hf_r, hb_s, hb_r, bs_s, bs_r, be_s, be_r, fs_s, fs_r, fe_s, fe_r,
    p_s, p_r, c_s, c_r, r_s, r_r, a_s, a_r,
):
    seq = lax.axis_index("seq")
    chan = lax.axis_index("chan")
    units = 2 * nt
    total = float(n_chan * nt * B)
    scale = float(n_seq * B) ** -0.5
    stride = n_seq // units
    owners_b = (0, stride, units)
    owners_f = (n_seq - 1 - stride * (units - 1), stride, units)
    sums_r = nt // 2 + 1
    owners_r = (0, n_seq // sums_r, sums_r)
    nz = 8 if n_seq % 8 == 0 else n_seq
    ny = n_seq // nz
    my_y, my_z = lax.div(seq, nz), lax.rem(seq, nz)

    def ring_order(i, n):
        return lax.rem(n // 2 + n + lax.div(i + 1, 2) * (1 - 2 * lax.rem(i, 2)), n)

    def far_first(i):
        dy, dz = ring_order(lax.rem(i, ny), ny), ring_order(lax.div(i, ny), nz)
        return lax.rem(my_y + dy, ny) * nz + lax.rem(my_z + dz, nz)

    def far_first_unit(i, count):
        wide = count // ny
        dy, dz = ring_order(lax.rem(i, ny), ny), ring_order(lax.div(i, ny), wide)
        return lax.rem(my_y + dy, ny) * wide + lax.rem(lax.div(my_z * wide, nz) + dz, wide)

    lane = lax.broadcasted_iota(jnp.int32, (B, B), 1)
    row = lax.broadcasted_iota(jnp.int32, (B, B), 0)
    lane_group = lane >> 4
    diag_groups = (row >> 4) == lane_group
    eye = row == lane

    def cols(k):
        return pl.ds(pl.multiple_of(k * B, B), B)

    def tile(ref, k):
        return ref[:, cols(k)].astype(F32)

    lane_s = lax.broadcasted_iota(jnp.int32, (GS, B), 1)
    row_s = lax.broadcasted_iota(jnp.int32, (GS, B), 0)
    group_s = lane_s >> 4

    def windows(ref, k):
        return jnp.concatenate([ref[k, a * GS:a * GS + W, :] for a in range(GT)], axis=1)

    def banded(bands, ref, k):
        full = dot(bands[k], windows(ref, k))
        blocks = []
        for a in range(GT):
            part = full[:, a * B:(a + 1) * B]
            out = part[0:GS]
            for g in range(1, GT):
                out = jnp.where(group_s == g, part[g * GS:(g + 1) * GS], out)
            blocks.append(out)
        return jnp.concatenate(blocks, axis=0)

    def squeeze(full):
        return jnp.sum(jnp.where(diag_groups, full, 0.0).reshape(GT, GS, B), axis=0)

    def remote(src, dst, ss, rs, axis, target):
        return pltpu.make_async_remote_copy(
            src_ref=src, dst_ref=dst, send_sem=ss, recv_sem=rs,
            device_id={axis: target}, device_id_type=MESH,
        )

    barrier = pltpu.get_barrier_semaphore()

    @pl.loop(0, n_seq - 1)
    def _(i):
        pl.semaphore_signal(barrier, inc=1, device_id={"seq": far_first(i)}, device_id_type=MESH)

    @pl.loop(1, n_chan)
    def _(d):
        pl.semaphore_signal(barrier, inc=1, device_id={"chan": lax.rem(chan + d, n_chan)}, device_id_type=MESH)

    fetches = [
        pltpu.make_async_copy(src, dst, in_sem.at[i])
        for i, (src, dst) in enumerate((
            (decay_in, decay), (cot_in, cot), (q_li_in, q_li), (k_mr_in, k_mr), (v_mr_in, v_mr),
            (resid_in, resid), (filt_in, filt), (gain_in, gain), (q_mr_in, q_mr), (k_li_in, k_li)))
    ]
    for fetch in fetches:
        fetch.start()

    time = lane.astype(F32)
    group_lane = lax.broadcasted_iota(jnp.int32, decay.shape, 1)

    def column(values, k):
        return jnp.concatenate([
            jnp.sum(jnp.where(group_lane == k * GT + g, values, 0.0), axis=1, keepdims=True) for g in range(GT)
        ], axis=0)

    for fetch in fetches[0:3]:
        fetch.wait()

    @pl.loop(0, nt, unroll=True)
    def _(k):
        hi, lo = split(jnp.exp(-column(decay[...], k) * time))
        back = (tile(cot, k) * tile(q_li, k)).astype(BF16)
        bli[k, 0:B, :] = back
        bli[k, B:2 * B, :] = jnp.zeros((B, B), BF16)
        xli[k, 0:B, :] = jnp.zeros((B, B), BF16)
        states = squeeze(dot(hi, back) + dot(lo, back))
        bs_src[2 * k] = states[0:8]
        bs_src[2 * k + 1] = states[8:16]

    for fetch in fetches[3:5]:
        fetch.wait()

    @pl.loop(0, nt, unroll=True)
    def _(k):
        ext[k, B:2 * B, :] = (tile(k_mr, k) * tile(v_mr, k)).astype(BF16)

    pl.semaphore_wait(barrier, n_seq - 1 + n_chan - 1)

    def owns(owners):
        base, step, count = owners
        place = seq - base
        return jnp.logical_and(jnp.logical_and(place >= 0, place < step * count), lax.rem(place, step) == 0)

    def unit(owners):
        return lax.div(seq - owners[0], owners[1])

    def send_unit(src, dst, ss, rs, owners, u):
        owner = owners[0] + owners[1] * u

        @pl.when(seq != owner)
        def _():
            remote(src.at[u], dst.at[seq], ss, rs, "seq", owner).start()

        @pl.when(seq == owner)
        def _():
            dst[seq] = src[u]

    def scatter(src, dst, ss, rs, owners):
        @pl.loop(0, owners[2])
        def _(i):
            send_unit(src, dst, ss, rs, owners, far_first_unit(i, owners[2]))

    def answer(e_src, e_dst, es, er, u, one):
        @pl.loop(0, n_seq - 1)
        def _(i):
            other = far_first(i)
            remote(e_src.at[0] if one else e_src.at[other], e_dst.at[u], es, er, "seq", other).start()

    def several(ref, ss, rs, count):
        return remote(ref.at[pl.ds(0, count)], ref.at[pl.ds(0, count)], ss, rs, "seq", lax.rem(seq + 1, n_seq))

    def but_own(owners, wait):
        count = owners[2]

        @pl.when(owns(owners))
        def _():
            wait(count - 1)

        @pl.when(jnp.logical_not(owns(owners)))
        def _():
            wait(count)

    def scatter_wait(src, ss, rs, owners):
        but_own(owners, lambda n: several(src, ss, rs, n).wait_send())

    def answer_wait(e_dst, es, er, owners):
        but_own(owners, lambda n: several(e_dst, es, er, n).wait_recv())

    def owner_wait(dst, ss, rs):
        several(dst, ss, rs, n_seq - 1).wait_recv()

    def owner_scan(dst, ss, rs, e_src, e_dst, es, er, owners, backward):
        @pl.when(owns(owners))
        def _():
            owner_wait(dst, ss, rs)
            u = unit(owners)
            fade = avec[u]

            def step(i, state):
                q = n_seq - 1 - i if backward else i
                e_src[q] = state
                return fade * state + dst[q]

            lax.fori_loop(0, n_seq, step, jnp.zeros((8, B), F32), unroll=8 if n_seq % 8 == 0 else 1)
            e_dst[u] = e_src[seq]
            answer(e_src, e_dst, es, er, u, False)

    scatter(bs_src, bs_dst, bs_s, bs_r, owners_b)

    def halo_f(k):
        return remote(ext.at[k, pl.ds(B, B)], ext.at[k, pl.ds(0, B)], hf_s, hf_r.at[k], "seq", lax.rem(seq + 1, n_seq))

    def halo_b(k):
        return remote(bext.at[k, pl.ds(0, B)], bext.at[k, pl.ds(B, B)], hb_s, hb_r.at[k], "seq",
                      lax.rem(seq + n_seq - 1, n_seq))

    @pl.when(seq < n_seq - 1)
    def _():
        @pl.loop(0, nt, unroll=True)
        def _(k):
            halo_f(k).start()

    @pl.when(seq == 0)
    def _():
        @pl.loop(0, nt, unroll=True)
        def _(k):
            ext[k, 0:B, :] = jnp.zeros((B, B), BF16)

    @pl.when(seq == n_seq - 1)
    def _():
        @pl.loop(0, nt, unroll=True)
        def _(k):
            bext[k, B:2 * B, :] = jnp.zeros((B, B), BF16)

    for fetch in fetches[5:]:
        fetch.wait()

    @pl.loop(0, nt, unroll=True)
    def _(k):
        rate = column(decay[...], k)
        weight = column(resid[...], k) * jnp.sqrt(2.0 * rate)
        fading = jnp.exp(-rate * time)
        powers = squeeze(jnp.broadcast_to(jnp.exp(-rate * float(B)), (B, B)))
        avec[2 * k] = powers[0:8]
        avec[2 * k + 1] = powers[8:16]
        taps[1, pl.ds(pl.multiple_of(k * GT, GT), GT), :] = jnp.sum((weight * fading).reshape(GT, GS, B), axis=1)
        hi, lo = split(jnp.exp(-rate * (B - 1.0 - time)))
        winf[k, 0:B, :] = hi
        winf[k, B:2 * B, :] = lo
        hi, lo = split((weight * jnp.exp(-rate * (B - time))).T)
        woutb[k, :, 0:B] = hi
        woutb[k, :, B:2 * B] = lo
        hi, lo = split((weight * jnp.exp(-rate * (time + 1.0))).T)
        woutf[k, :, 0:B] = hi
        woutf[k, :, B:2 * B] = lo

    reflect = jnp.where(row == ((B - lane) & (B - 1)), 1.0, 0.0)
    taps[0] = filt[...].astype(BF16).astype(F32)
    for which in range(2):
        rtaps[which] = dot(taps[which].astype(BF16), reflect.astype(BF16))

    @pl.loop(0, nt, unroll=True)
    def _(k):
        for ref, which, keep, out in (
            (taps, 1, lane_s >= row_s, tlb), (rtaps, 0, lane_s > row_s, tmf),
            (taps, 0, lane_s >= row_s, tmb), (rtaps, 1, lane_s > row_s, tlf),
        ):
            for g in range(GT):
                line = jnp.broadcast_to(ref[which, pl.ds(k * GT + g, 1), :], (GS, B))
                matrix = pltpu.roll(line, 0, axis=1, stride=1, stride_axis=0)
                out[k, g * GS:(g + 1) * GS, 0:B] = jnp.where(keep, matrix, 0.0).astype(BF16)
                out[k, g * GS:(g + 1) * GS, B:W] = jnp.where(keep, 0.0, matrix)[:, 0:GS].astype(BF16)

    def carried(wout, e_dst, k):
        state = jnp.concatenate([e_dst[2 * k], e_dst[2 * k + 1]], axis=0)
        hi, lo = split(jnp.where(diag_groups, jnp.concatenate([state] * GT, axis=0), 0.0))
        return dot(wout[k], jnp.concatenate([hi, hi], axis=0)) + dot(wout[k, :, 0:B], lo)

    @pl.loop(0, nt, unroll=True)
    def _(k):
        gml[k] = banded(tlb, bli, k)

    owner_scan(bs_dst, bs_s, bs_r, be_src, be_dst, be_s, be_r, owners_b, True)

    squares = jnp.zeros((B, B), F32)

    def mr_step(k, squares):
        @pl.when(seq > 0)
        def _():
            halo_f(k).wait_recv()

        value = banded(tmf, ext, k)
        conv[k] = value
        gated = (tile(q_mr, k) * value).astype(BF16).astype(F32)
        outm[k] = gated
        return squares + gated * gated

    squares = lax.fori_loop(0, nt, mr_step, squares, unroll=True)

    def as_row(partial):
        column = jnp.sum(partial, axis=1, keepdims=True)
        return jnp.sum(jnp.where(eye, column, 0.0), axis=0, keepdims=True)

    def as_column(line):
        return jnp.sum(jnp.where(eye, line, 0.0), axis=1, keepdims=True)

    def all_of(buf, ss, rs):
        part = buf.at[pl.ds(0, n_chan - 1), pl.ds(0, 1)]
        return remote(part, part, ss, rs, "chan", lax.rem(chan + 1, n_chan))

    def psum_start(buf, partial, ss, rs):
        buf[chan, 0:1, :] = as_row(partial)
        mine = buf.at[chan, pl.ds(0, 1)]

        @pl.loop(0, n_chan - 1)
        def _(i):
            remote(mine, mine, ss, rs, "chan", lax.rem(chan + ring_order(i, n_chan), n_chan)).start()

    def psum_end(buf, ss, rs):
        all_of(buf, ss, rs).wait_recv()
        sums = buf[0, 0:1, :]
        for c in range(1, n_chan):
            sums = sums + buf[c, 0:1, :]
        return sums

    psum_start(pbuf, squares, p_s, p_r)
    answer_wait(be_dst, be_s, be_r, owners_b)

    def li_step(k, cross):
        grad = gml[k] + carried(woutb, be_dst, k)
        gml[k] = grad
        return cross + grad * tile(k_li, k) * outm[k] * gain[pl.ds(k, 1), :]

    cross = lax.fori_loop(0, nt, li_step, jnp.zeros((B, B), F32), unroll=True)
    psum_start(cbuf, cross, c_s, c_r)

    inv_row = lax.rsqrt(psum_end(pbuf, p_s, p_r) / total + 1e-06)
    inv = as_column(inv_row)

    @pl.loop(0, nt, unroll=True)
    def _(k):
        normed = outm[k] * inv * gain[pl.ds(k, 1), :]
        mixed = (tile(k_li, k) * normed).astype(BF16)
        xli[k, B:2 * B, :] = mixed
        both = dot(winf[k], mixed)
        states = squeeze(both[0:B] + both[B:2 * B])
        fs_src[2 * k] = states[0:8]
        fs_src[2 * k + 1] = states[8:16]

    scatter(fs_src, fs_dst, fs_s, fs_r, owners_f)

    gains = []
    for k in range(nt):
        grad, scaled = gml[k], outm[k] * inv
        g_kli[:, cols(k)] = (grad * (scaled * gain[pl.ds(k, 1), :])).astype(BF16)
        gains.append(jnp.sum(grad * tile(k_li, k) * scaled, axis=0, keepdims=True))
        cli[k] = banded(tlf, xli, k)
    gains.append(jnp.zeros((16 - nt, B), F32))
    r_src[nt // 2] = jnp.concatenate(gains, axis=0).astype(BF16)
    send_unit(r_src, r_dst, r_s, r_r, owners_r, nt // 2)

    pull = as_column(inv_row * inv_row * inv_row * psum_end(cbuf, c_s, c_r) / total)

    @pl.loop(0, nt, unroll=True)
    def _(k):
        grad_out = inv * (gml[k] * tile(k_li, k) * gain[pl.ds(k, 1), :]) - outm[k] * pull
        bext[k, 0:B, :] = (grad_out * tile(q_mr, k)).astype(BF16)

        g_qmr[:, cols(k)] = (grad_out * conv[k]).astype(BF16)

    row64 = lax.broadcasted_iota(jnp.int32, (8 * GT, B), 0)

    halves = []
    for k in range(nt):
        back = bext[k, 0:B, :]
        masked = jnp.concatenate([
            jnp.concatenate([
                jnp.where(group_s == g, back[a * GS:(a + 1) * GS], jnp.zeros((GS, B), BF16)) for a in range(GT)
            ], axis=1) for g in range(GT)
        ], axis=0)
        gram = lax.dot_general(masked, windows(ext, k), (((1,), (1,)), ((), ())), preferred_element_type=F32)
        wrapped = jnp.concatenate([gram[:, B:W], jnp.zeros((B, B - GS), F32)], axis=1)
        cyclic = jnp.where(lane <= (row & (GS - 1)), wrapped, gram[:, 0:B])
        sums = [
            cyclic[g * GS:g * GS + 8] + pltpu.roll(cyclic[g * GS + 8:(g + 1) * GS], B - 8, axis=1) for g in range(GT)
        ]
        acc = jnp.concatenate(sums, axis=0)
        for bit in range(3):
            acc = jnp.where(((row64 >> bit) & 1) == 1, pltpu.roll(acc, B - (1 << bit), axis=1), acc)
        halves.append(jnp.sum(acc.reshape(GT, 8, B), axis=1))
        if k % 2:
            r_src[k // 2] = jnp.concatenate(halves[-2:], axis=0).astype(BF16)
            send_unit(r_src, r_dst, r_s, r_r, owners_r, k // 2)

    owner_scan(fs_dst, fs_s, fs_r, fe_src, fe_dst, fe_s, fe_r, owners_f, False)

    @pl.when(seq > 0)
    def _():
        @pl.loop(0, nt)
        def _(k):
            halo_b(k).start()

    @pl.when(owns(owners_r))
    def _():
        owner_wait(r_dst, r_s, r_r)
        u = unit(owners_r)
        result = jnp.sum(r_dst[...].astype(F32), axis=0).astype(BF16)
        a_src[0] = result
        a_dst[u] = result
        answer(a_src, a_dst, a_s, a_r, u, True)

    answer_wait(fe_dst, fe_s, fe_r, owners_f)

    @pl.loop(0, nt, unroll=True)
    def _(k):
        value = cli[k] + carried(woutf, fe_dst, k)
        out_li[:, cols(k)] = (tile(q_li, k) * value).astype(BF16)
        g_qli[:, cols(k)] = (tile(cot, k) * value).astype(BF16)

    @pl.loop(0, nt, unroll=True)
    def _(k):
        @pl.when(seq < n_seq - 1)
        def _():
            halo_b(k).wait_recv()

        grad = banded(tmb, bext, k)
        g_kmr[:, cols(k)] = (grad * tile(v_mr, k)).astype(BF16)
        g_vmr[:, cols(k)] = (grad * tile(k_mr, k)).astype(BF16)

    answer_wait(a_dst, a_s, a_r, owners_r)
    sums = jnp.concatenate([a_dst[u] for u in range(nt // 2)], axis=0)
    g_filt[...] = dot(sums, reflect.astype(BF16)) * scale
    g_gain[...] = a_dst[nt // 2].astype(F32)[0:nt] * scale

    @pl.when(seq < n_seq - 1)
    def _():
        remote(ext.at[:, pl.ds(B, B)], ext.at[:, pl.ds(0, B)], hf_s, hf_r.at[0], "seq", lax.rem(seq + 1, n_seq)).wait_send()

    @pl.when(seq > 0)
    def _():
        remote(bext.at[:, pl.ds(0, B)], bext.at[:, pl.ds(B, B)], hb_s, hb_r.at[0], "seq",
               lax.rem(seq + n_seq - 1, n_seq)).wait_send()

    scatter_wait(bs_src, bs_s, bs_r, owners_b)
    scatter_wait(fs_src, fs_s, fs_r, owners_f)
    scatter_wait(r_src, r_s, r_r, owners_r)
    for e_src, es, er, owners in ((be_src, be_s, be_r, owners_b), (fe_src, fe_s, fe_r, owners_f)):
        @pl.when(owns(owners))
        def _():
            several(e_src, es, er, n_seq - 1).wait_send()

    @pl.when(owns(owners_r))
    def _():
        several(r_dst, a_s, a_r, n_seq - 1).wait_send()

    all_of(pbuf, p_s, p_r).wait_send()
    all_of(cbuf, c_s, c_r).wait_send()


def deliver(*refs):
    count = len(refs) // 2
    sem = refs[-1]
    copies = [pltpu.make_async_copy(refs[i], refs[count + i], sem.at[i]) for i in range(count)]
    for copy in copies:
        copy.start()
    for copy in copies:
        copy.wait()


def solution(mesh):
    n_seq, n_chan = mesh.shape["seq"], mesh.shape["chan"]

    def on_device(q_mr, k_mr, v_mr, q_li, k_li, cot, filt, gain, decay, resid):
        rows, width = q_mr.shape
        nt = width // B
        units = 2 * nt
        groups, taps_count = filt.shape
        vmem = pl.BlockSpec(memory_space=pltpu.VMEM)
        hbm = pl.BlockSpec(memory_space=pltpu.HBM)
        dma = pltpu.SemaphoreType.DMA
        one = dma(())
        state = lambda count: pltpu.VMEM((count, 8, B), F32)
        part = lambda count: pltpu.VMEM((count, 16, B), BF16)
        plane = lambda kind: pltpu.VMEM((nt, B, B), kind)
        arguments = [
            pltpu.with_memory_space_constraint(value, pltpu.HBM)
            for value in (q_mr, k_mr, v_mr, q_li, k_li, cot, filt, gain.reshape(nt, B), decay.T, resid.T)
        ]
        shapes = [((rows, width), BF16)] * 6 + [((nt, B), F32), ((groups, taps_count), F32)]
        outs = pl.pallas_call(
            functools.partial(kernel, n_seq, n_chan, nt),
            out_shape=[jax.ShapeDtypeStruct(*shape) for shape in shapes],
            in_specs=[hbm] * 10,
            out_specs=[vmem] * 8,
            scratch_shapes=[pltpu.VMEM(value.shape, value.dtype) for value in arguments] + [
                pltpu.VMEM((nt, 2 * B, B), BF16), pltpu.VMEM((nt, 2 * B, B), BF16),
                pltpu.VMEM((nt, B, W), BF16), pltpu.VMEM((nt, B, W), BF16),
                pltpu.VMEM((nt, B, W), BF16), pltpu.VMEM((nt, B, W), BF16),
                plane(F32), plane(F32), plane(F32), pltpu.VMEM((nt, 2 * B, B), BF16), pltpu.VMEM((nt, 2 * B, B), BF16), plane(F32),
                pltpu.VMEM((nt, 2 * B, B), BF16),
                pltpu.VMEM((nt, B, 2 * B), BF16), pltpu.VMEM((nt, B, 2 * B), BF16),
                pltpu.VMEM((2, nt * GT, B), F32), pltpu.VMEM((2, nt * GT, B), F32), state(units),
                state(units), state(n_seq), state(n_seq), state(units),
                state(units), state(n_seq), state(n_seq), state(units),
                state(n_chan), state(n_chan), part(nt // 2 + 1), part(n_seq), part(1), part(nt // 2 + 1),
                dma((10,)), one, dma((nt,)), one, dma((nt,)),
                one, one, one, one, one, one, one, one, one, one, one, one, one, one, one, one,
            ],
            compiler_params=pltpu.CompilerParams(
                collective_id=0, has_side_effects=True, vmem_limit_bytes=40 * 1024 * 1024
            ),
        )(*arguments)
        outs = pl.pallas_call(
            deliver,
            out_shape=[jax.ShapeDtypeStruct(*shape) for shape in shapes],
            in_specs=[vmem] * 8,
            out_specs=[hbm] * 8,
            scratch_shapes=[dma((8,))],
            compiler_params=pltpu.CompilerParams(vmem_limit_bytes=1024 * 1024),
        )(*outs)
        return (*outs[:6], outs[6].reshape(width), outs[7])

    wide, by_group, by_chan = P("seq", "chan"), P("chan", None), P("chan")
    return jax.shard_map(
        on_device, mesh=mesh,
        in_specs=(wide,) * 6 + (by_group, by_chan, by_group, by_group),
        out_specs=(wide,) * 6 + (by_chan, by_group),
        check_vma=False,
    )
```
